256 devices in a mesh: tm: 64 (over z, y, core), head: 4 (over x).
Axes of the slice: x: 4, y: 4, z: 8, core: 2. Of those that a mesh axis runs over, the one named last changes fastest.
Arguments:
- video_qkv: bfloat16 [3, 32768, 3072], P(None, 'tm', 'head'), may hold values from -1600 to 1600
- audio_qkv: bfloat16 [3, 64, 256, 3072], P(None, None, 'tm', 'head'), may hold values from -1600 to 1600
- video_gain: float32 [2, 3072], P(None, 'head'), may hold values from 1 to 2
- audio_gain: float32 [2, 3072], P(None, 'head'), may hold values from 1 to 2
- video_cot: bfloat16 [32768, 3072], P('tm', 'head'), may hold values from -6 to 6
- audio_cot: bfloat16 [64, 256, 3072], P(None, 'tm', 'head'), may hold values from -6 to 6
- intersection: int32 [4096, 2], replicated, may hold values from 0 to 255, as said below
- lengths: int32 [4096], replicated, may hold values from 1 to 4, as said below
Outputs:
- out_video: bfloat16 [32768, 3072], P('tm', 'head')
- out_audio: bfloat16 [64, 256, 3072], P(None, 'tm', 'head')
- grad_video: bfloat16 [3, 32768, 3072], P(None, 'tm', 'head')
- grad_audio: bfloat16 [3, 64, 256, 3072], P(None, None, 'tm', 'head')
The draws below stay inside these ranges and needn't reach their ends.
Inputs may be any that keep to these rules, and one draw needn't show every extreme that they name: With c = g * 4 // 64, intersection[g, 0] is c or c - 1 and intersection[g, 1] is c or c + 1, both within the clip's video blocks. `lengths`: some blocks are full.
All inputs are finite; a program needn't handle non-finite values.
Results may differ from the reference program's by a relative error of at most 0.007.
The reference program's roundings to bfloat16 on the way count: a program that leaves them out, or rounds other values in their place, can miss the bound.
Values may be sent and summed in bfloat16 or wider, within the bound.
A program may use at most 128 MiB of HBM per device.

```python
import jax
import jax.numpy as jnp
from jax import lax

HEADS = 24
HD = 128
VB = 4
VBLK = 128
ABLK = 4
FEAT = 3072
NV = 256
NA = 4096
VTOK = 32768
NH = 16
HA = 64
N_TM = 64


def draw_video_qkv(key, part):
    key = jax.random.fold_in(key, 1)
    base_key, row_key = jax.random.split(key)
    column = jnp.arange(FEAT, dtype=jnp.float32) / FEAT
    base_draw = jax.random.truncated_normal(base_key, -4.0, 4.0, (3, VTOK, FEAT))
    spread = 10.0
    row_scale = jnp.exp(jax.random.uniform(row_key, (2, VTOK, 1)) * jnp.log(spread))
    scaled = base_draw[:2] * row_scale * spread ** column
    return jnp.concatenate([scaled, base_draw[2:]], 0).astype(jnp.bfloat16)


def draw_audio_qkv(key, part):
    key = jax.random.fold_in(key, 2)
    base_key, row_key = jax.random.split(key)
    column = jnp.arange(FEAT, dtype=jnp.float32) / FEAT
    base_draw = jax.random.truncated_normal(base_key, -4.0, 4.0, (3, NA, ABLK, FEAT))
    spread = 10.0
    row_scale = jnp.exp(jax.random.uniform(row_key, (2, NA, ABLK, 1)) * jnp.log(spread))
    scaled = base_draw[:2] * row_scale * spread ** column
    whole = jnp.concatenate([scaled, base_draw[2:]], 0)
    return whole.reshape(3, N_TM, N_TM * ABLK, FEAT).astype(jnp.bfloat16)


def draw_intersection(key, part):
    key = jax.random.fold_in(key, 3)
    center = jnp.arange(NA, dtype=jnp.int32) * VB // N_TM
    reach = jax.random.randint(key, (2, NA), 0, 2)
    lowest = jnp.maximum(center - reach[0], 0)
    highest = jnp.minimum(center + reach[1], NV - 1)
    return jnp.stack([lowest, highest], -1).astype(jnp.int32)


def draw_lengths(key, part):
    key = jax.random.fold_in(key, 4)
    full_key, size_key = jax.random.split(key)
    is_full = (jax.random.randint(full_key, (NA,), 0, 4) == 0) | (jnp.arange(NA) == 0)
    random_len = jax.random.randint(size_key, (NA,), 1, ABLK + 1)
    return jnp.where(is_full, ABLK, random_len).astype(jnp.int32)


def steps_of(key, shape, cuts, low, top_value):
    loudness, own = 1.0, jax.random.fold_in(key, 6)
    for axis_at, shards_of in cuts:
        draws = jnp.exp(jax.random.uniform(jax.random.fold_in(own, axis_at), (shards_of,), jnp.float32, low / len(cuts), top_value / len(cuts)))
        loudness = loudness * jnp.repeat(draws, shape[axis_at] // shards_of).reshape([-1 if axis == axis_at else 1 for axis in range(len(shape))])
    return loudness


def scatter_about(key, dims, width, most, cuts=(), kind=jnp.bfloat16):
    values = width * jax.random.normal(key, dims, jnp.float32)
    if cuts:
        values = values * steps_of(key, dims, cuts, -0.22, 0.18)
    return jnp.clip(values, -most, most).astype(kind)


def setup_inputs(seed: int = 0) -> dict:
    seeds = jax.random.split(jax.random.key(seed), 9)
    return {
        "video_qkv": draw_video_qkv(jax.random.fold_in(seeds[8], 71), 0),
        "audio_qkv": draw_audio_qkv(jax.random.fold_in(seeds[8], 71), 0),
        "video_gain": jnp.clip(1.0 + 1.0 * jax.random.uniform(seeds[2], (2, FEAT), jnp.float32) ** steps_of(seeds[2], (2, FEAT), ((1, 4),), -0.2, 0.2), 1.0, 2.0),
        "audio_gain": jnp.clip(1.0 + 1.0 * jax.random.uniform(seeds[3], (2, FEAT), jnp.float32) ** steps_of(seeds[3], (2, FEAT), ((1, 4),), -0.2, 0.2), 1.0, 2.0),
        "video_cot": scatter_about(seeds[4], (VTOK, FEAT), 1.0, 6.0, ((0, 64), (1, 4))),
        "audio_cot": scatter_about(seeds[5], (N_TM, N_TM * ABLK, FEAT), 1.0, 6.0, ((1, 64), (2, 4))),
        "intersection": draw_intersection(jax.random.fold_in(seeds[8], 71), 0),
        "lengths": draw_lengths(jax.random.fold_in(seeds[8], 71), 0),
    }


EPSILON = 1e-06
NEGATIVE = -1e+30

def attend(queries, keyset, values, paired, cotangent):
    softmax_scale = queries.shape[-1] ** (-0.5)
    scores = jnp.einsum('qhe,khe->hqk', queries.astype(jnp.float32), keyset.astype(jnp.float32)) * softmax_scale
    scores = jnp.where(paired[None], scores, NEGATIVE)
    row_max = lax.optimization_barrier(jnp.max(scores, -1, keepdims=True))
    exponent = jnp.exp(scores - row_max)
    attention = (exponent / lax.optimization_barrier(jnp.sum(exponent, -1, keepdims=True))).astype(jnp.bfloat16)
    widened = lax.optimization_barrier(attention).astype(jnp.float32)
    output = jnp.einsum('hqk,khe->qhe', widened, values.astype(jnp.float32))
    value_grad = jnp.einsum('hqk,qhe->khe', widened, cotangent.astype(jnp.float32))
    prob_grad = jnp.einsum('qhe,khe->hqk', cotangent.astype(jnp.float32), values.astype(jnp.float32))
    score_grad = (widened * (prob_grad - lax.optimization_barrier(jnp.sum(prob_grad * widened, -1, keepdims=True)))).astype(jnp.bfloat16)
    score_wide = score_grad.astype(jnp.float32)
    query_grad = jnp.einsum('hqk,khe->qhe', score_wide, keyset.astype(jnp.float32)) * softmax_scale
    key_grad = jnp.einsum('hqk,qhe->khe', score_wide, queries.astype(jnp.float32)) * softmax_scale
    return (output, query_grad, key_grad, value_grad)

def to_heads(array):
    return array.reshape(array.shape[0], -1, HD)

def to_rows(array):
    return array.reshape(array.shape[0], -1)

def cross_window(position, video_query, video_pairs, video_cotangent, audio_query, audio_pairs, audio_cotangent, low_table, high_table, live_table, sub_blocks, video_block, audio_block, edge_blocks):
    video_rows = video_query.shape[0]
    audio_rows = audio_query.shape[0]
    video_sub = position * sub_blocks + jnp.arange(video_rows, dtype=jnp.int32) // video_block
    key_low = jnp.repeat(low_table, audio_block)
    key_high = jnp.repeat(high_table, audio_block)
    key_live = jnp.arange(key_low.shape[0], dtype=jnp.int32) % audio_block < jnp.repeat(live_table, audio_block)
    paired_va = (key_low[None] <= video_sub[:, None]) & (video_sub[:, None] <= key_high[None]) & key_live[None]
    start = edge_blocks * audio_block
    query_low = key_low[start:start + audio_rows]
    query_high = key_high[start:start + audio_rows]
    query_live = key_live[start:start + audio_rows]
    key_sub = position * sub_blocks - 1 + jnp.arange(video_pairs.shape[1], dtype=jnp.int32) // video_block
    paired_av = (query_low[:, None] <= key_sub[None]) & (key_sub[None] <= query_high[:, None])
    cot_live = jnp.where(query_live[:, None], audio_cotangent, jnp.zeros_like(audio_cotangent))
    out_va, dq_video, dk_audio, dv_audio = attend(to_heads(video_query), to_heads(audio_pairs[0]), to_heads(audio_pairs[1]), paired_va, to_heads(video_cotangent))
    out_av, dq_audio, dk_video, dv_video = attend(to_heads(audio_query), to_heads(video_pairs[0]), to_heads(video_pairs[1]), paired_av, to_heads(cot_live))
    audio_out = to_rows(out_av).astype(jnp.bfloat16)
    audio_out = jnp.where(query_live[:, None], audio_out, jnp.zeros_like(audio_out))
    return (to_rows(out_va).astype(jnp.bfloat16), audio_out, to_rows(dq_video), jnp.stack([to_rows(dk_video), to_rows(dv_video)]), to_rows(dq_audio), jnp.stack([to_rows(dk_audio), to_rows(dv_audio)]))

def fold_windows(extended, margin):
    center = extended[:, :, margin:extended.shape[2] - margin]
    row_count = center.shape[2]
    blank = jnp.zeros_like(extended[:1, :, :margin])
    from_prev = jnp.concatenate([blank, extended[:-1, :, extended.shape[2] - margin:]], 0)
    from_next = jnp.concatenate([extended[1:, :, :margin], blank], 0)
    total = center + jnp.pad(from_prev, ((0, 0), (0, 0), (0, row_count - margin), (0, 0)))
    total = total + jnp.pad(from_next, ((0, 0), (0, 0), (row_count - margin, 0), (0, 0)))
    return jnp.moveaxis(total, 1, 0).reshape(2, -1, total.shape[-1])

def reference(video_qkv, audio_qkv, video_gain, audio_gain, video_cot, audio_cot, intersection, lengths):
    feat_all = HEADS * HD
    video_rows = VB * VBLK
    audio_rows = N_TM * ABLK
    video_raw = video_qkv[:2].astype(jnp.float32)
    video_rate = lax.rsqrt(lax.optimization_barrier(jnp.sum(video_raw * video_raw, -1)) / feat_all + EPSILON)
    video_normed = (video_raw * video_rate[..., None] * video_gain[:, None, :]).astype(jnp.bfloat16)
    audio_flat = audio_qkv.reshape(3, NA * ABLK, FEAT)
    cot_flat = audio_cot.reshape(NA * ABLK, FEAT)
    audio_raw = audio_flat[:2].astype(jnp.float32)
    audio_rate = lax.rsqrt(lax.optimization_barrier(jnp.sum(audio_raw * audio_raw, -1)) / feat_all + EPSILON)
    audio_normed = (audio_raw * audio_rate[..., None] * audio_gain[:, None, :]).astype(jnp.bfloat16)
    video_padded = jnp.pad(jnp.stack([video_normed[1], video_qkv[2]]), ((0, 0), (VBLK, VBLK), (0, 0)))
    audio_padded = jnp.pad(jnp.stack([audio_normed[1], audio_flat[2]]), ((0, 0), (HA, HA), (0, 0)))
    low_padded = jnp.pad(intersection[:, 0], (NH, NH), constant_values=1073741824)
    high_padded = jnp.pad(intersection[:, 1], (NH, NH), constant_values=-1)
    live_padded = jnp.pad(lengths, (NH, NH), constant_values=0)

    def one_window(position):
        video_query = lax.dynamic_slice_in_dim(video_normed[0], position * video_rows, video_rows, 0)
        video_pairs = lax.dynamic_slice_in_dim(video_padded, position * video_rows, video_rows + 2 * VBLK, 1)
        video_cotangent = lax.dynamic_slice_in_dim(video_cot, position * video_rows, video_rows, 0)
        audio_query = lax.dynamic_slice_in_dim(audio_normed[0], position * audio_rows, audio_rows, 0)
        audio_pairs = lax.dynamic_slice_in_dim(audio_padded, position * audio_rows, audio_rows + 2 * HA, 1)
        audio_cotangent = lax.dynamic_slice_in_dim(cot_flat, position * audio_rows, audio_rows, 0)
        low_table = lax.dynamic_slice_in_dim(low_padded, position * N_TM, N_TM + 2 * NH, 0)
        high_table = lax.dynamic_slice_in_dim(high_padded, position * N_TM, N_TM + 2 * NH, 0)
        live_table = lax.dynamic_slice_in_dim(live_padded, position * N_TM, N_TM + 2 * NH, 0)
        return cross_window(position, video_query, video_pairs, video_cotangent, audio_query, audio_pairs, audio_cotangent, low_table, high_table, live_table, VB, VBLK, ABLK, NH)
    results = lax.map(one_window, jnp.arange(N_TM, dtype=jnp.int32))
    out_video = results[0].reshape(VTOK, FEAT)
    out_audio = results[1].reshape(N_TM, N_TM * ABLK, FEAT)
    video_kv_grad = fold_windows(results[3], VBLK)
    audio_kv_grad = fold_windows(results[5], HA)
    audio_in = jnp.concatenate([results[4].reshape(1, NA * ABLK, FEAT), audio_kv_grad], 0).astype(jnp.bfloat16)
    audio_in = lax.optimization_barrier(audio_in)
    video_in = jnp.stack([results[2].reshape(VTOK, FEAT), video_kv_grad[0]])
    video_inner = lax.optimization_barrier(jnp.sum(video_raw * video_gain[:, None, :] * video_in, -1))
    video_back = video_gain[:, None, :] * video_in * video_rate[..., None] - video_raw * (video_rate ** 3 * video_inner / feat_all)[..., None]
    grad_video = jnp.concatenate([video_back, video_kv_grad[1:2]], 0).astype(jnp.bfloat16)
    audio_wide = audio_in[:2].astype(jnp.float32)
    audio_inner = lax.optimization_barrier(jnp.sum(audio_raw * audio_gain[:, None, :] * audio_wide, -1))
    audio_back = audio_gain[:, None, :] * audio_wide * audio_rate[..., None] - audio_raw * (audio_rate ** 3 * audio_inner / feat_all)[..., None]
    grad_audio = jnp.concatenate([audio_back.astype(jnp.bfloat16), audio_in[2:3]], 0).reshape(3, N_TM, N_TM * ABLK, FEAT)
    return (out_video, out_audio, grad_video, grad_audio)
```

```python
import functools

import jax
import jax.numpy as jnp
from jax import lax
from jax.experimental import pallas as pl
from jax.experimental.pallas import tpu as pltpu
from jax.sharding import PartitionSpec as P

HEADS = 24
HD = 128
VB = 4
VBLK = 128
CHUNKS = 3

EPSILON = 1e-06
NEGATIVE = -1e30
MESH = pl.DeviceIdType.MESH
F32 = jnp.float32
BF16 = jnp.bfloat16


def mm(a, b, ca, cb):
    return lax.dot_general(a, b, (((ca,), (cb,)), ((), ())), preferred_element_type=F32)


def attend(query, key, value, cot, bias):
    scale = HD ** (-0.5)
    scores = mm(key, query, 1, 1) * scale + bias
    exponent = jnp.exp(scores - jnp.max(scores, 0, keepdims=True))
    inverse = 1.0 / jnp.sum(exponent, 0, keepdims=True)
    probs = (exponent * inverse).astype(BF16)
    wide = probs.astype(F32)
    prob_grad = mm(value, cot, 1, 1)
    inner = jnp.sum(prob_grad * wide, 0, keepdims=True)
    score_grad = (wide * (prob_grad - inner)).astype(BF16)
    out = mm(probs, value, 0, 0)
    query_grad = mm(score_grad, key, 0, 0) * scale
    key_grad = mm(score_grad, query, 1, 0) * scale
    value_grad = mm(probs, cot, 1, 0)
    return out, query_grad, key_grad, value_grad


def iota(shape, dim):
    return lax.broadcasted_iota(jnp.int32, shape, dim)


def to_row(column):
    n = column.shape[0]
    return jnp.sum(jnp.where(iota((n, 128), 0) == iota((n, 128), 1), column, 0.0), 0, keepdims=True)


def to_column(row, n):
    return jnp.sum(jnp.where(iota((n, 128), 0) == iota((n, 128), 1), row, 0.0), 1, keepdims=True)


def kernel(
    dims,
    vq_hbm, aq_hbm, vg, ag, vc_hbm, ac_hbm, inter, lens,
    ov_hbm, oa, gv_hbm, ga,
    vraw, vcot, araw, acot, vqn, vkv, msg, win, aqn, akv, acw,
    ov, dqv, dvkv, dqa, dakv, oaw, evs, evr, eas, ear, ret, retr, aun, gv,
    vab, avb, live, stats, rates, inner,
    in_sem, out_sem, st_send, st_recv, vh_send, vh_recv, ah_send, ah_recv,
    a2a_send, a2a_recv, ev_send, ev_recv, ea_send, ea_recv, ret_send, ret_recv,
):
    n, x, f = dims
    c_all, w = CHUNKS, f // CHUNKS
    heads = w // HD
    tok = 4
    nb = n // VB
    ga_rows = nb * tok
    a_rows = n * tok
    ae_rows = a_rows + 2 * ga_rows
    v_rows = VB * VBLK
    lv, la = min(128, v_rows), min(128, a_rows)
    nv, na = v_rows // lv, a_rows // la
    blocks = n * n
    feat_all = HEADS * HD
    me = lax.axis_index("tm")
    hd = lax.axis_index("head")
    left, right = lax.rem(me + n - 1, n), lax.rem(me + 1, n)

    barrier = pltpu.get_barrier_semaphore()
    for k in range(1, x):
        pl.semaphore_signal(barrier, inc=1, device_id={"head": lax.rem(hd + k, x)}, device_id_type=MESH)

    def greet(k, carry):
        pl.semaphore_signal(barrier, inc=1, device_id={"tm": lax.rem(me + k, n)}, device_id_type=MESH)
        return carry

    loads = [
        pltpu.make_async_copy(vq_hbm.at[pl.ds(0, 2)], vraw, in_sem.at[0]),
        pltpu.make_async_copy(aq_hbm, araw, in_sem.at[1]),
        pltpu.make_async_copy(ac_hbm, acot, in_sem.at[2]),
        pltpu.make_async_copy(vq_hbm.at[2], vkv.at[1, pl.ds(VBLK, v_rows)], in_sem.at[3]),
        pltpu.make_async_copy(vc_hbm, vcot, in_sem.at[4]),
    ]
    for load in loads:
        load.start()
    lax.fori_loop(1, n, greet, 0)

    start = me * n - nb
    count = blocks // 128
    chunk_0 = lax.rem((start + blocks) // 128, count)
    chunk_1 = lax.rem(chunk_0 + 1, count)
    rows = iota((ae_rows, 1), 0)
    block = start + lax.shift_right_logical(rows, 2)
    block = jnp.where(block < 0, block + blocks, block)
    block = jnp.where(block >= blocks, block - blocks, block)
    tables = []
    for ref, at in ((inter, 0), (inter, 1), (lens, 0)):
        column = jnp.zeros((ae_rows, 1), F32)
        for chunk in (chunk_0, chunk_1):
            lanes = pl.ds(pl.multiple_of(chunk * 128, 128), 128)
            values = ref[at : at + 1, lanes].astype(F32)
            hit = (chunk * 128 + iota((ae_rows, 128), 1)) == block
            column = column + jnp.sum(jnp.where(hit, values, 0.0), 1, keepdims=True)
        tables.append(column)
    low, high, length = tables
    is_live = jnp.bitwise_and(rows, 3).astype(F32) < length
    first = (me * VB).astype(F32)
    for b in range(VB):
        span = slice(b * ga_rows, (b + 3) * ga_rows)
        ok = (low[span] <= first + b) & (first + b <= high[span]) & is_live[span]
        vab[b] = jnp.broadcast_to(jnp.where(ok, 0.0, NEGATIVE), (3 * ga_rows, VBLK))
    pair = 2 * ga_rows
    for p in range(2):
        span = slice(ga_rows + p * pair, ga_rows + (p + 1) * pair)
        low_row = to_row(low[span])[:, :pair]
        high_row = to_row(high[span])[:, :pair]
        for e in range(4):
            at = first + (2 * p + e - 1)
            ok = (low_row <= at) & (at <= high_row)
            avb[p, e * VBLK : (e + 1) * VBLK] = jnp.broadcast_to(
                jnp.where(ok, 0.0, NEGATIVE), (VBLK, pair)
            )
    live[...] = jnp.broadcast_to(
        jnp.where(is_live[ga_rows : ga_rows + a_rows], 1.0, 0.0), (a_rows, 128)
    )

    stats[0, hd] = jnp.zeros((16, 128), F32)
    loads[1].wait()
    for p in range(2):
        for i in range(na):
            cut = slice(i * la // tok, (i + 1) * la // tok)
            raw = araw[p, cut].reshape(la, f).astype(F32)
            at = 2 * nv + p * na + i
            stats[0, hd, at : at + 1] = to_row(jnp.sum(raw * raw, 1, keepdims=True))
    loads[0].wait()
    for p in range(2):
        for i in range(nv):
            raw = vraw[p, i * lv : (i + 1) * lv].astype(F32)
            at = p * nv + i
            stats[0, hd, at : at + 1] = to_row(jnp.sum(raw * raw, 1, keepdims=True))
    loads[2].wait()
    loads[3].wait()
    loads[4].wait()

    def share(turn):
        copies = []
        for k in range(1, x):
            copies.append(
                pltpu.make_async_remote_copy(
                    stats.at[turn, hd], stats.at[turn, hd],
                    st_send.at[turn], st_recv.at[turn],
                    device_id={"head": lax.rem(hd + k, x)}, device_id_type=MESH,
                )
            )
        for copy in copies:
            copy.start()

    def shared(turn):
        some = stats.at[turn, pl.ds(0, x - 1)]
        pltpu.make_async_copy(some, some, st_recv.at[turn]).wait()
        pltpu.make_async_copy(some, some, st_send.at[turn]).wait()
        total = stats[turn, 0]
        for k in range(1, x):
            total = total + stats[turn, k]
        return total

    def edge_copy(src, dst, send, recv, to):
        return pltpu.make_async_remote_copy(
            src, dst, send, recv, device_id={"tm": to}, device_id_type=MESH
        )

    pl.semaphore_wait(barrier, n - 1 + x - 1)
    share(0)

    def video_halo(kind):
        return (
            edge_copy(vkv.at[kind, pl.ds(VBLK, VBLK)], vkv.at[kind, pl.ds(VBLK + v_rows, VBLK)],
                      vh_send.at[kind, 0], vh_recv.at[kind, 0], left),
            edge_copy(vkv.at[kind, pl.ds(v_rows, VBLK)], vkv.at[kind, pl.ds(0, VBLK)],
                      vh_send.at[kind, 1], vh_recv.at[kind, 1], right),
        )

    for copy in video_halo(1):
        copy.start()
    rates[...] = lax.rsqrt(shared(0) / feat_all + EPSILON)

    size = 4 * ga_rows
    one, two = iota((size, size), 0), iota((size, size), 1)

    def moved(row):
        arr = lax.rem(lax.div(row, tok), 4)
        return arr * ga_rows + lax.div(row, 4 * tok) * tok + lax.rem(row, tok)

    pack = jnp.where(two == moved(one), 1.0, 0.0).astype(BF16)
    unpack = jnp.where(one == moved(two), 1.0, 0.0).astype(BF16)

    def audio_rate(p, row_at, row_count):
        i, off = divmod(row_at, la)
        at = 2 * nv + p * na + i
        return to_column(rates[at : at + 1], la)[off : off + row_count]

    for j in range(VB):
        cut = slice(j * nb, (j + 1) * nb)
        parts = []
        for p in range(2):
            raw = araw[p, cut].reshape(ga_rows, f).astype(F32)
            normed = raw * audio_rate(p, j * ga_rows, ga_rows) * ag[p : p + 1]
            parts.append(normed.astype(BF16))
        parts.append(araw[2, cut].reshape(ga_rows, f))
        parts.append(acot[cut].reshape(ga_rows, f))
        packed = mm(pack, jnp.concatenate(parts, 0), 1, 0).astype(BF16)
        msg[cut] = packed.reshape(nb, 16, f)

    def lanes_of(c):
        return pl.ds(pl.multiple_of(c * w, w), w)

    def spread(src, dst, send, recv):
        def chunk(c, carry):
            lanes = lanes_of(c)

            def one_device(k, inner_carry):
                d = lax.rem(me + k, n)
                edge_copy(src.at[d, :, lanes], dst.at[me, :, lanes], send.at[c], recv.at[c], d).start()
                return inner_carry

            lax.fori_loop(1, n, one_device, 0)
            pltpu.make_async_copy(src.at[me, :, lanes], dst.at[me, :, lanes], recv.at[c]).start()
            return carry

        return chunk

    def landed(dst, recv, c):
        some = dst.at[:, :, lanes_of(c)]
        pltpu.make_async_copy(some, some, recv.at[c]).wait()

    def sent(src, send, c):
        some = src.at[pl.ds(0, n - 1), :, lanes_of(c)]
        pltpu.make_async_copy(some, some, send.at[c]).wait()

    lax.fori_loop(0, c_all, spread(msg, win, a2a_send, a2a_recv), 0)

    for p in (1, 0):
        for i in range(nv):
            cut = slice(i * lv, (i + 1) * lv)
            at = p * nv + i
            raw = vraw[p, cut].astype(F32)
            normed = (raw * to_column(rates[at : at + 1], lv) * vg[p : p + 1]).astype(BF16)
            if p == 1:
                vkv[0, VBLK + i * lv : VBLK + (i + 1) * lv] = normed
            else:
                vqn[cut] = normed
        if p == 1:
            for copy in video_halo(0):
                copy.start()

    def audio_halo(c):
        lanes = lanes_of(c)
        return (
            edge_copy(akv.at[:, pl.ds(ga_rows, ga_rows), lanes],
                      akv.at[:, pl.ds(ga_rows + a_rows, ga_rows), lanes],
                      ah_send.at[c, 0], ah_recv.at[c, 0], left),
            edge_copy(akv.at[:, pl.ds(a_rows, ga_rows), lanes],
                      akv.at[:, pl.ds(0, ga_rows), lanes],
                      ah_send.at[c, 1], ah_recv.at[c, 1], right),
        )

    def grad_halo(src, dst, send, recv, c):
        lanes = lanes_of(c)
        return (
            edge_copy(src.at[0, :, :, lanes], dst.at[1, :, :, lanes], send.at[c, 0], recv.at[c, 0], left),
            edge_copy(src.at[1, :, :, lanes], dst.at[0, :, :, lanes], send.at[c, 1], recv.at[c, 1], right),
        )

    spread_back = spread(ret, retr, ret_send, ret_recv)

    def finish(c):
        lanes = lanes_of(c)
        for copy in grad_halo(eas, ear, ea_send, ea_recv, c):
            copy.wait_recv()
        for j in range(VB):
            cut = slice(j * ga_rows, (j + 1) * ga_rows)
            parts = [dqa[cut, lanes]]
            for kind in range(2):
                total = dakv[kind, (j + 1) * ga_rows : (j + 2) * ga_rows, lanes]
                if j == 0:
                    total = total + ear[0, kind, :, lanes].astype(F32)
                if j == VB - 1:
                    total = total + ear[1, kind, :, lanes].astype(F32)
                parts.append(total.astype(BF16))
            parts.append(oaw[cut, lanes])
            packed = mm(pack, jnp.concatenate(parts, 0), 1, 0).astype(BF16)
            ret[j * nb : (j + 1) * nb, :, lanes] = packed.reshape(nb, 16, w)
        spread_back(c, 0)

    def chunk_work(c, carry):
        lanes = lanes_of(c)
        landed(win, a2a_recv, c)
        for j in range(VB):
            some = win[j * nb : (j + 1) * nb, :, lanes].reshape(size, w)
            some = mm(unpack, some, 1, 0)
            cut = slice(j * ga_rows, (j + 1) * ga_rows)
            ext = slice((j + 1) * ga_rows, (j + 2) * ga_rows)
            aqn[cut, lanes] = some[:ga_rows].astype(BF16)
            akv[0, ext, lanes] = some[ga_rows : 2 * ga_rows].astype(BF16)
            akv[1, ext, lanes] = some[2 * ga_rows : 3 * ga_rows].astype(BF16)
            acw[cut, lanes] = jnp.where(live[cut, :1] > 0.0, some[3 * ga_rows :], 0.0).astype(BF16)
        for copy in audio_halo(c):
            copy.start()

        @pl.when(c == 0)
        def _():
            for kind in range(2):
                for copy in video_halo(kind):
                    copy.wait_recv()

        for h in range(heads):
            at = pl.ds(pl.multiple_of(c * w + h * HD, HD), HD)
            sums = [[None] * 6, [None] * 6]
            for p in range(2):
                cut = slice(p * pair, (p + 1) * pair)
                ext = slice(2 * p * VBLK, (2 * p + 4) * VBLK)
                out, dq, dk, dv = attend(
                    aqn[cut, at], vkv[0, ext, at], vkv[1, ext, at], acw[cut, at], avb[p]
                )
                oaw[cut, at] = jnp.where(live[cut, :1] > 0.0, out, 0.0).astype(BF16)
                dqa[cut, at] = dq.astype(BF16)
                for kind, grad in enumerate((dk, dv)):
                    for e in range(4):
                        term = grad[e * VBLK : (e + 1) * VBLK]
                        old = sums[kind][2 * p + e]
                        sums[kind][2 * p + e] = term if old is None else old + term
            for kind in range(2):
                evs[0, kind, :, at] = sums[kind][0].astype(BF16)
                evs[1, kind, :, at] = sums[kind][5].astype(BF16)
                for e in range(4):
                    dvkv[kind, e * VBLK : (e + 1) * VBLK, at] = sums[kind][e + 1]
        for copy in grad_halo(evs, evr, ev_send, ev_recv, c):
            copy.start()
        for copy in audio_halo(c):
            copy.wait_recv()
        for h in range(heads):
            at = pl.ds(pl.multiple_of(c * w + h * HD, HD), HD)
            sums = [[None] * 6, [None] * 6]
            for b in range(VB):
                cut = slice(b * VBLK, (b + 1) * VBLK)
                ext = slice(b * ga_rows, (b + 3) * ga_rows)
                out, dq, dk, dv = attend(
                    vqn[cut, at], akv[0, ext, at], akv[1, ext, at], vcot[cut, at], vab[b]
                )
                ov[cut, at] = out.astype(BF16)
                dqv[cut, at] = dq
                for kind, grad in enumerate((dk, dv)):
                    for e in range(3):
                        term = grad[e * ga_rows : (e + 1) * ga_rows]
                        old = sums[kind][b + e]
                        sums[kind][b + e] = term if old is None else old + term
            for kind in range(2):
                eas[0, kind, :, at] = sums[kind][0].astype(BF16)
                eas[1, kind, :, at] = sums[kind][5].astype(BF16)
                for e in range(4):
                    dakv[kind, (e + 1) * ga_rows : (e + 2) * ga_rows, at] = sums[kind][e + 1]
        for copy in grad_halo(eas, ear, ea_send, ea_recv, c):
            copy.start()

        @pl.when(c > 0)
        def _():
            finish(c - 1)

        return carry

    lax.fori_loop(0, c_all, chunk_work, 0)
    put_ov = pltpu.make_async_copy(ov, ov_hbm, out_sem.at[0])
    put_ov.start()
    finish(c_all - 1)

    def wait_edges(c, carry):
        for copy in grad_halo(evs, evr, ev_send, ev_recv, c):
            copy.wait_recv()
        return carry

    lax.fori_loop(0, c_all, wait_edges, 0)
    for kind in range(2):
        head_rows, tail_rows = slice(0, VBLK), slice(v_rows - VBLK, v_rows)
        dvkv[kind, head_rows] = dvkv[kind, head_rows] + evr[0, kind].astype(F32)
        dvkv[kind, tail_rows] = dvkv[kind, tail_rows] + evr[1, kind].astype(F32)
    stats[1, hd] = jnp.zeros((16, 128), F32)
    for p in range(2):
        for i in range(nv):
            cut = slice(i * lv, (i + 1) * lv)
            grad = dqv[cut] if p == 0 else dvkv[0, cut]
            term = vraw[p, cut].astype(F32) * vg[p : p + 1] * grad
            at = p * nv + i
            stats[1, hd, at : at + 1] = to_row(jnp.sum(term, 1, keepdims=True))
    share(1)
    for i in range(nv):
        cut = slice(i * lv, (i + 1) * lv)
        gv[2, cut] = dvkv[1, cut].astype(BF16)
    inner[...] = rates[...] * rates[...] * rates[...] * shared(1) / feat_all
    for p in range(2):
        for i in range(nv):
            cut = slice(i * lv, (i + 1) * lv)
            at = p * nv + i
            grad = dqv[cut] if p == 0 else dvkv[0, cut]
            rate = to_column(rates[at : at + 1], lv)
            back = vg[p : p + 1] * grad * rate - vraw[p, cut].astype(F32) * to_column(inner[at : at + 1], lv)
            gv[p, cut] = back.astype(BF16)
    put_gv = pltpu.make_async_copy(gv, gv_hbm, out_sem.at[1])
    put_gv.start()

    def take(c, carry):
        lanes = lanes_of(c)
        landed(retr, ret_recv, c)
        for j in range(VB):
            some = retr[j * nb : (j + 1) * nb, :, lanes].reshape(size, w)
            some = mm(unpack, some, 1, 0).astype(BF16)
            for arr in range(4):
                aun[arr, j * ga_rows : (j + 1) * ga_rows, lanes] = some[arr * ga_rows : (arr + 1) * ga_rows]
        return carry

    lax.fori_loop(0, c_all, take, 0)
    stats[2, hd] = jnp.zeros((16, 128), F32)
    for p in range(2):
        for i in range(na):
            cut = slice(i * la, (i + 1) * la)
            raw = araw[p, i * la // tok : (i + 1) * la // tok].reshape(la, f).astype(F32)
            term = raw * ag[p : p + 1] * aun[p, cut].astype(F32)
            at = 2 * nv + p * na + i
            stats[2, hd, at : at + 1] = to_row(jnp.sum(term, 1, keepdims=True))
    share(2)
    ga[2] = aun[2].reshape(n, tok, f)
    oa[...] = aun[3].reshape(n, tok, f)
    inner[...] = rates[...] * rates[...] * rates[...] * shared(2) / feat_all
    for p in range(2):
        for i in range(na):
            cut = slice(i * la, (i + 1) * la)
            owned = slice(i * la // tok, (i + 1) * la // tok)
            at = 2 * nv + p * na + i
            raw = araw[p, owned].reshape(la, f).astype(F32)
            back = (
                ag[p : p + 1] * aun[p, cut].astype(F32) * to_column(rates[at : at + 1], la)
                - raw * to_column(inner[at : at + 1], la)
            )
            ga[p, owned] = back.astype(BF16).reshape(la // tok, tok, f)

    for kind in range(2):
        for copy in video_halo(kind):
            copy.wait_send()

    def drain(c, carry):
        sent(msg, a2a_send, c)
        sent(ret, ret_send, c)
        for copy in audio_halo(c) + grad_halo(evs, evr, ev_send, ev_recv, c) + grad_halo(eas, ear, ea_send, ea_recv, c):
            copy.wait_send()
        return carry

    lax.fori_loop(0, c_all, drain, 0)
    put_ov.wait()
    put_gv.wait()


def local(video_qkv, audio_qkv, video_gain, audio_gain, video_cot, audio_cot, intersection, lengths):
    n, x = lax.axis_size("tm"), lax.axis_size("head")
    f = video_qkv.shape[2]
    v_rows, a_rows = video_qkv.shape[1], n * audio_qkv.shape[2]
    ga_rows = a_rows // VB
    ae_rows, ve_rows = a_rows + 2 * ga_rows, v_rows + 2 * VBLK
    hbm = pl.BlockSpec(memory_space=pltpu.HBM)
    vmem = pl.BlockSpec(memory_space=pltpu.VMEM)
    dma = pltpu.SemaphoreType.DMA
    bf = lambda *shape: pltpu.VMEM(shape, BF16)
    f32 = lambda *shape: pltpu.VMEM(shape, F32)
    scratch = [
        bf(2, v_rows, f), bf(v_rows, f), bf(3, n, 4, f), bf(n, 4, f),
        bf(v_rows, f), bf(2, ve_rows, f), bf(n, 16, f), bf(n, 16, f),
        bf(a_rows, f), bf(2, ae_rows, f), bf(a_rows, f),
        bf(v_rows, f), f32(v_rows, f), f32(2, v_rows, f),
        bf(a_rows, f), f32(2, ae_rows, f), bf(a_rows, f),
        bf(2, 2, VBLK, f), bf(2, 2, VBLK, f), bf(2, 2, ga_rows, f), bf(2, 2, ga_rows, f),
        bf(n, 16, f), bf(n, 16, f), bf(4, a_rows, f), bf(3, v_rows, f),
        f32(VB, 3 * ga_rows, VBLK), f32(2, 4 * VBLK, 2 * ga_rows), f32(a_rows, 128),
        f32(3, x, 16, 128), f32(16, 128), f32(16, 128),
        dma((5,)), dma((2,)), dma((3,)), dma((3,)), dma((2, 2)), dma((2, 2)),
        dma((CHUNKS, 2)), dma((CHUNKS, 2)), dma((CHUNKS,)), dma((CHUNKS,)),
        dma((CHUNKS, 2)), dma((CHUNKS, 2)), dma((CHUNKS, 2)), dma((CHUNKS, 2)),
        dma((CHUNKS,)), dma((CHUNKS,)),
    ]
    out_video, out_audio, grad_video, grad_audio = pl.pallas_call(
        functools.partial(kernel, (n, x, f)),
        out_shape=(
            jax.ShapeDtypeStruct(video_cot.shape, BF16),
            jax.ShapeDtypeStruct(audio_cot.shape, BF16),
            jax.ShapeDtypeStruct(video_qkv.shape, BF16),
            jax.ShapeDtypeStruct(audio_qkv.shape, BF16),
        ),
        in_specs=[hbm, hbm, vmem, vmem, hbm, hbm, vmem, vmem],
        out_specs=(hbm, vmem, hbm, vmem),
        scratch_shapes=scratch,
        compiler_params=pltpu.CompilerParams(
            collective_id=0, has_side_effects=True, vmem_limit_bytes=56 << 20
        ),
        name="window",
    )(
        video_qkv, audio_qkv, video_gain, audio_gain, video_cot, audio_cot,
        intersection.T, lengths[None],
    )
    return out_video, out_audio, grad_video, grad_audio


def solution(mesh):
    return jax.shard_map(
        local,
        mesh=mesh,
        in_specs=(
            P(None, "tm", "head"),
            P(None, None, "tm", "head"),
            P(None, "head"),
            P(None, "head"),
            P("tm", "head"),
            P(None, "tm", "head"),
            P(),
            P(),
        ),
        out_specs=(
            P("tm", "head"),
            P(None, "tm", "head"),
            P(None, "tm", "head"),
            P(None, None, "tm", "head"),
        ),
        check_vma=False,
    )
```

```python
import functools

import jax
import jax.numpy as jnp
from jax import lax
from jax.experimental import pallas as pl
from jax.experimental.pallas import tpu as pltpu
from jax.sharding import PartitionSpec as P

HEADS = 24
HD = 128
VB = 4
VBLK = 128
CHUNKS = 3

EPSILON = 1e-06
NEGATIVE = -1e30
MESH = pl.DeviceIdType.MESH
F32 = jnp.float32
BF16 = jnp.bfloat16


def mm(a, b, ca, cb):
    return lax.dot_general(a, b, (((ca,), (cb,)), ((), ())), preferred_element_type=F32)


def attend(query, key, value, cot, bias):
    scale = HD ** (-0.5)
    scores = mm(key, query, 1, 1) * scale + bias
    exponent = jnp.exp(scores - jnp.max(scores, 0, keepdims=True))
    inverse = 1.0 / jnp.sum(exponent, 0, keepdims=True)
    probs = (exponent * inverse).astype(BF16)
    wide = probs.astype(F32)
    prob_grad = mm(value, cot, 1, 1)
    inner = jnp.sum(prob_grad * wide, 0, keepdims=True)
    score_grad = (wide * (prob_grad - inner)).astype(BF16)
    out = mm(probs, value, 0, 0)
    query_grad = mm(score_grad, key, 0, 0) * scale
    key_grad = mm(score_grad, query, 1, 0) * scale
    value_grad = mm(probs, cot, 1, 0)
    return out, query_grad, key_grad, value_grad


def iota(shape, dim):
    return lax.broadcasted_iota(jnp.int32, shape, dim)


def to_row(column):
    n = column.shape[0]
    return jnp.sum(jnp.where(iota((n, 128), 0) == iota((n, 128), 1), column, 0.0), 0, keepdims=True)


def to_column(row, n):
    return jnp.sum(jnp.where(iota((n, 128), 0) == iota((n, 128), 1), row, 0.0), 1, keepdims=True)


def kernel(
    dims,
    vq_hbm, aq_hbm, vg_hbm, ag_hbm, vc_hbm, ac_hbm, inter_hbm, lens_hbm,
    ov, oa, gv, ga,
    vg, ag, inter, lens, vraw, vcot, araw, acot, vqn, vkv, msg, win, aqn, akv, acw,
    dqv, dvkv, dqa, dakv, oaw, evs, evr, eas, ear, ret, retr, aun,
    vab, avb, live, stats, rates, inner,
    in_sem, st_send, st_recv, vh_send, vh_recv, ah_send, ah_recv,
    a2a_send, a2a_recv, ev_send, ev_recv, ea_send, ea_recv, ret_send, ret_recv,
):
    n, x, f = dims
    c_all, w = CHUNKS, f // CHUNKS
    heads = w // HD
    tok = 4
    nb = n // VB
    ga_rows = nb * tok
    a_rows = n * tok
    ae_rows = a_rows + 2 * ga_rows
    v_rows = VB * VBLK
    lv, la = min(128, v_rows), min(128, a_rows)
    nv, na = v_rows // lv, a_rows // la
    blocks = n * n
    feat_all = HEADS * HD
    me = lax.axis_index("tm")
    hd = lax.axis_index("head")
    left, right = lax.rem(me + n - 1, n), lax.rem(me + 1, n)

    barrier = pltpu.get_barrier_semaphore()
    for k in range(1, x):
        pl.semaphore_signal(barrier, inc=1, device_id={"head": lax.rem(hd + k, x)}, device_id_type=MESH)

    def greet(k, carry):
        pl.semaphore_signal(barrier, inc=1, device_id={"tm": lax.rem(me + k, n)}, device_id_type=MESH)
        return carry

    loads = [
        pltpu.make_async_copy(vq_hbm.at[pl.ds(0, 2)], vraw, in_sem.at[0]),
        pltpu.make_async_copy(aq_hbm, araw, in_sem.at[1]),
        pltpu.make_async_copy(ac_hbm, acot, in_sem.at[2]),
        pltpu.make_async_copy(vq_hbm.at[2], vkv.at[1, pl.ds(VBLK, v_rows)], in_sem.at[3]),
        pltpu.make_async_copy(vc_hbm, vcot, in_sem.at[4]),
        pltpu.make_async_copy(inter_hbm, inter, in_sem.at[5]),
        pltpu.make_async_copy(lens_hbm, lens, in_sem.at[6]),
        pltpu.make_async_copy(vg_hbm, vg, in_sem.at[7]),
        pltpu.make_async_copy(ag_hbm, ag, in_sem.at[8]),
    ]
    for load in loads:
        load.start()
    lax.fori_loop(1, n, greet, 0)

    start = me * n - nb
    count = blocks // 128
    chunk_0 = lax.rem((start + blocks) // 128, count)
    chunk_1 = lax.rem(chunk_0 + 1, count)
    rows = iota((ae_rows, 1), 0)
    block = start + lax.shift_right_logical(rows, 2)
    block = jnp.where(block < 0, block + blocks, block)
    block = jnp.where(block >= blocks, block - blocks, block)
    loads[5].wait()
    loads[6].wait()
    tables = []
    for ref, at in ((inter, 0), (inter, 1), (lens, 0)):
        column = jnp.zeros((ae_rows, 1), F32)
        for chunk in (chunk_0, chunk_1):
            lanes = pl.ds(pl.multiple_of(chunk * 128, 128), 128)
            values = ref[at : at + 1, lanes].astype(F32)
            hit = (chunk * 128 + iota((ae_rows, 128), 1)) == block
            column = column + jnp.sum(jnp.where(hit, values, 0.0), 1, keepdims=True)
        tables.append(column)
    low, high, length = tables
    is_live = jnp.bitwise_and(rows, 3).astype(F32) < length
    first = (me * VB).astype(F32)
    for b in range(VB):
        span = slice(b * ga_rows, (b + 3) * ga_rows)
        ok = (low[span] <= first + b) & (first + b <= high[span]) & is_live[span]
        vab[b] = jnp.broadcast_to(jnp.where(ok, 0.0, NEGATIVE), (3 * ga_rows, VBLK))
    pair = 2 * ga_rows
    for p in range(2):
        span = slice(ga_rows + p * pair, ga_rows + (p + 1) * pair)
        low_row = to_row(low[span])[:, :pair]
        high_row = to_row(high[span])[:, :pair]
        for e in range(4):
            at = first + (2 * p + e - 1)
            ok = (low_row <= at) & (at <= high_row)
            avb[p, e * VBLK : (e + 1) * VBLK] = jnp.broadcast_to(
                jnp.where(ok, 0.0, NEGATIVE), (VBLK, pair)
            )
    live[...] = jnp.broadcast_to(
        jnp.where(is_live[ga_rows : ga_rows + a_rows], 1.0, 0.0), (a_rows, 128)
    )

    stats[0, hd] = jnp.zeros((16, 128), F32)
    loads[1].wait()
    for p in range(2):
        for i in range(na):
            cut = slice(i * la // tok, (i + 1) * la // tok)
            raw = araw[p, cut].reshape(la, f).astype(F32)
            at = 2 * nv + p * na + i
            stats[0, hd, at : at + 1] = to_row(jnp.sum(raw * raw, 1, keepdims=True))
    loads[0].wait()
    for p in range(2):
        for i in range(nv):
            raw = vraw[p, i * lv : (i + 1) * lv].astype(F32)
            at = p * nv + i
            stats[0, hd, at : at + 1] = to_row(jnp.sum(raw * raw, 1, keepdims=True))
    for i in (2, 3, 4, 7, 8):
        loads[i].wait()

    def share(turn):
        copies = []
        for k in range(1, x):
            copies.append(
                pltpu.make_async_remote_copy(
                    stats.at[turn, hd], stats.at[turn, hd],
                    st_send.at[turn], st_recv.at[turn],
                    device_id={"head": lax.rem(hd + k, x)}, device_id_type=MESH,
                )
            )
        for copy in copies:
            copy.start()

    def shared(turn):
        some = stats.at[turn, pl.ds(0, x - 1)]
        pltpu.make_async_copy(some, some, st_recv.at[turn]).wait()
        pltpu.make_async_copy(some, some, st_send.at[turn]).wait()
        total = stats[turn, 0]
        for k in range(1, x):
            total = total + stats[turn, k]
        return total

    def edge_copy(src, dst, send, recv, to):
        return pltpu.make_async_remote_copy(
            src, dst, send, recv, device_id={"tm": to}, device_id_type=MESH
        )

    size = 4 * ga_rows
    one, two = iota((size, size), 0), iota((size, size), 1)

    def moved(row):
        arr = lax.rem(lax.div(row, tok), 4)
        return arr * ga_rows + lax.div(row, 4 * tok) * tok + lax.rem(row, tok)

    pack = jnp.where(two == moved(one), 1.0, 0.0).astype(BF16)
    unpack = jnp.where(one == moved(two), 1.0, 0.0).astype(BF16)

    def lane(c, h):
        return slice(c * w + h * HD, c * w + (h + 1) * HD)

    def put_messages(dst, kind, c, j, arrays):
        parts = [array[:, lane(c, h)] for h in range(heads) for array in arrays]
        packed = mm(pack, jnp.concatenate(parts, 0), 1, 0).astype(BF16)
        dst[kind, c, j * nb : (j + 1) * nb] = packed.reshape(nb, 16, HD)

    for j in range(VB):
        cut = slice(j * nb, (j + 1) * nb)
        arrays = araw[2, cut].reshape(ga_rows, f), acot[cut].reshape(ga_rows, f)
        for c in range(c_all):
            put_messages(msg, 0, c, j, arrays)

    pl.semaphore_wait(barrier, n - 1 + x - 1)
    share(0)

    def video_halo(kind):
        return (
            edge_copy(vkv.at[kind, pl.ds(VBLK, VBLK)], vkv.at[kind, pl.ds(VBLK + v_rows, VBLK)],
                      vh_send.at[kind, 0], vh_recv.at[kind, 0], left),
            edge_copy(vkv.at[kind, pl.ds(v_rows, VBLK)], vkv.at[kind, pl.ds(0, VBLK)],
                      vh_send.at[kind, 1], vh_recv.at[kind, 1], right),
        )

    for copy in video_halo(1):
        copy.start()

    def lanes_of(c):
        return pl.ds(pl.multiple_of(c * w, w), w)

    def spread(src, dst, send, recv):
        def chunk(kind, c):
            def one_device(k, carry):
                d = lax.rem(me + k, n)
                edge_copy(src.at[kind, c, d], dst.at[kind, c, me], send.at[kind, c], recv.at[kind, c], d).start()
                return carry

            lax.fori_loop(1, n, one_device, 0)
            pltpu.make_async_copy(src.at[kind, c, me], dst.at[kind, c, me], recv.at[kind, c]).start()

        return chunk

    def landed(dst, recv, kind, c):
        some = dst.at[kind, c]
        pltpu.make_async_copy(some, some, recv.at[kind, c]).wait()

    def sent(src, send, kind, c):
        some = src.at[kind, c, pl.ds(0, n - 1)]
        pltpu.make_async_copy(some, some, send.at[kind, c]).wait()

    spread_out = spread(msg, win, a2a_send, a2a_recv)
    spread_back = spread(ret, retr, ret_send, ret_recv)

    def each_chunk(fn):
        def body(c, carry):
            fn(c)
            return carry

        lax.fori_loop(0, c_all, body, 0)

    each_chunk(lambda c: spread_out(0, c))
    rates[...] = lax.rsqrt(shared(0) / feat_all + EPSILON)

    def audio_rate(p, row_at, row_count):
        i, off = divmod(row_at, la)
        at = 2 * nv + p * na + i
        return to_column(rates[at : at + 1], la)[off : off + row_count]

    for p in (1, 0):
        for i in range(nv):
            cut = slice(i * lv, (i + 1) * lv)
            at = p * nv + i
            raw = vraw[p, cut].astype(F32)
            normed = (raw * to_column(rates[at : at + 1], lv) * vg[p : p + 1]).astype(BF16)
            if p == 1:
                vkv[0, VBLK + i * lv : VBLK + (i + 1) * lv] = normed
            else:
                vqn[cut] = normed
        if p == 1:
            for copy in video_halo(0):
                copy.start()

    for j in range(VB):
        cut = slice(j * nb, (j + 1) * nb)
        arrays = []
        for p in range(2):
            raw = araw[p, cut].reshape(ga_rows, f).astype(F32)
            normed = raw * audio_rate(p, j * ga_rows, ga_rows) * ag[p : p + 1]
            arrays.append(normed.astype(BF16))
        for c in range(c_all):
            put_messages(msg, 1, c, j, arrays)
    each_chunk(lambda c: spread_out(1, c))

    def audio_halo(kind, c):
        lanes = lanes_of(c)
        return (
            edge_copy(akv.at[kind, pl.ds(ga_rows, ga_rows), lanes],
                      akv.at[kind, pl.ds(ga_rows + a_rows, ga_rows), lanes],
                      ah_send.at[kind, c, 0], ah_recv.at[kind, c, 0], left),
            edge_copy(akv.at[kind, pl.ds(a_rows, ga_rows), lanes],
                      akv.at[kind, pl.ds(0, ga_rows), lanes],
                      ah_send.at[kind, c, 1], ah_recv.at[kind, c, 1], right),
        )

    def grad_halo(src, dst, send, recv, c):
        lanes = lanes_of(c)
        return (
            edge_copy(src.at[0, :, :, lanes], dst.at[1, :, :, lanes], send.at[c, 0], recv.at[c, 0], left),
            edge_copy(src.at[1, :, :, lanes], dst.at[0, :, :, lanes], send.at[c, 1], recv.at[c, 1], right),
        )

    def lane_at(c, h):
        return pl.ds(pl.multiple_of(c * w + h * HD, HD), HD)

    def finish(c):
        for copy in grad_halo(eas, ear, ea_send, ea_recv, c):
            copy.wait_recv()
        for j in range(VB):
            cut = slice(j * ga_rows, (j + 1) * ga_rows)
            ext = slice((j + 1) * ga_rows, (j + 2) * ga_rows)
            parts = [], []
            for h in range(heads):
                at = lane_at(c, h)
                grads = []
                for kind in range(2):
                    total = dakv[kind, ext, at]
                    if j == 0:
                        total = total + ear[0, kind, :, at].astype(F32)
                    if j == VB - 1:
                        total = total + ear[1, kind, :, at].astype(F32)
                    grads.append(total.astype(BF16))
                parts[0].extend((oaw[cut, at], grads[1]))
                parts[1].extend((dqa[cut, at], grads[0]))
            for kind in range(2):
                packed = mm(pack, jnp.concatenate(parts[kind], 0), 1, 0).astype(BF16)
                ret[kind, c, j * nb : (j + 1) * nb] = packed.reshape(nb, 16, HD)

    def unpacked(src, kind, c, j):
        rows = src[kind, c, j * nb : (j + 1) * nb].reshape(size, HD)
        return mm(unpack, rows, 1, 0)

    def take_values(c):
        landed(win, a2a_recv, 0, c)
        for j in range(VB):
            some = unpacked(win, 0, c, j)
            cut = slice(j * ga_rows, (j + 1) * ga_rows)
            ext = slice((j + 1) * ga_rows, (j + 2) * ga_rows)
            for h in range(heads):
                at = lane_at(c, h)
                top = 2 * h * ga_rows
                akv[1, ext, at] = some[top : top + ga_rows].astype(BF16)
                cots = some[top + ga_rows : top + 2 * ga_rows]
                acw[cut, at] = jnp.where(live[cut, :1] > 0.0, cots, 0.0).astype(BF16)
        for copy in audio_halo(1, c):
            copy.start()

    each_chunk(take_values)
    for kind in range(2):
        for copy in video_halo(kind):
            copy.wait_recv()

    def chunk_work(c):
        landed(win, a2a_recv, 1, c)
        for j in range(VB):
            some = unpacked(win, 1, c, j)
            cut = slice(j * ga_rows, (j + 1) * ga_rows)
            ext = slice((j + 1) * ga_rows, (j + 2) * ga_rows)
            for h in range(heads):
                at = lane_at(c, h)
                top = 2 * h * ga_rows
                aqn[cut, at] = some[top : top + ga_rows].astype(BF16)
                akv[0, ext, at] = some[top + ga_rows : top + 2 * ga_rows].astype(BF16)
        for copy in audio_halo(0, c):
            copy.start()

        for h in range(heads):
            at = lane_at(c, h)
            sums = [[None] * 6, [None] * 6]
            for p in range(2):
                cut = slice(p * pair, (p + 1) * pair)
                ext = slice(2 * p * VBLK, (2 * p + 4) * VBLK)
                out, dq, dk, dv = attend(
                    aqn[cut, at], vkv[0, ext, at], vkv[1, ext, at], acw[cut, at], avb[p]
                )
                oaw[cut, at] = jnp.where(live[cut, :1] > 0.0, out, 0.0).astype(BF16)
                dqa[cut, at] = dq.astype(BF16)
                for kind, grad in enumerate((dk, dv)):
                    for e in range(4):
                        term = grad[e * VBLK : (e + 1) * VBLK]
                        old = sums[kind][2 * p + e]
                        sums[kind][2 * p + e] = term if old is None else old + term
            for kind in range(2):
                evs[0, kind, :, at] = sums[kind][0].astype(BF16)
                evs[1, kind, :, at] = sums[kind][5].astype(BF16)
                for e in range(4):
                    dvkv[kind, e * VBLK : (e + 1) * VBLK, at] = sums[kind][e + 1]
        for copy in grad_halo(evs, evr, ev_send, ev_recv, c):
            copy.start()

        @pl.when(c > 0)
        def _():
            finish(c - 1)
            spread_back(1, c - 1)

        @pl.when(c == 1)
        def _():
            spread_back(0, 0)

        for kind in range(2):
            for copy in audio_halo(kind, c):
                copy.wait_recv()
        for h in range(heads):
            at = lane_at(c, h)
            sums = [[None] * 6, [None] * 6]
            for b in range(VB):
                cut = slice(b * VBLK, (b + 1) * VBLK)
                ext = slice(b * ga_rows, (b + 3) * ga_rows)
                out, dq, dk, dv = attend(
                    vqn[cut, at], akv[0, ext, at], akv[1, ext, at], vcot[cut, at], vab[b]
                )
                ov[cut, at] = out.astype(BF16)
                dqv[cut, at] = dq
                for kind, grad in enumerate((dk, dv)):
                    for e in range(3):
                        term = grad[e * ga_rows : (e + 1) * ga_rows]
                        old = sums[kind][b + e]
                        sums[kind][b + e] = term if old is None else old + term
            for kind in range(2):
                eas[0, kind, :, at] = sums[kind][0].astype(BF16)
                eas[1, kind, :, at] = sums[kind][5].astype(BF16)
                for e in range(4):
                    dakv[kind, (e + 1) * ga_rows : (e + 2) * ga_rows, at] = sums[kind][e + 1]
        for copy in grad_halo(eas, ear, ea_send, ea_recv, c):
            copy.start()

    each_chunk(chunk_work)
    finish(c_all - 1)
    spread_back(1, c_all - 1)
    for c in range(1, c_all):
        spread_back(0, c)

    def wait_edges(c):
        for copy in grad_halo(evs, evr, ev_send, ev_recv, c):
            copy.wait_recv()

    each_chunk(wait_edges)
    for kind in range(2):
        head_rows, tail_rows = slice(0, VBLK), slice(v_rows - VBLK, v_rows)
        dvkv[kind, head_rows] = dvkv[kind, head_rows] + evr[0, kind].astype(F32)
        dvkv[kind, tail_rows] = dvkv[kind, tail_rows] + evr[1, kind].astype(F32)
    stats[1, hd] = jnp.zeros((16, 128), F32)
    for p in range(2):
        for i in range(nv):
            cut = slice(i * lv, (i + 1) * lv)
            grad = dqv[cut] if p == 0 else dvkv[0, cut]
            term = vraw[p, cut].astype(F32) * vg[p : p + 1] * grad
            at = p * nv + i
            stats[1, hd, at : at + 1] = to_row(jnp.sum(term, 1, keepdims=True))
    share(1)
    for i in range(nv):
        cut = slice(i * lv, (i + 1) * lv)
        gv[2, cut] = dvkv[1, cut].astype(BF16)
    inner[...] = rates[...] * rates[...] * rates[...] * shared(1) / feat_all
    for p in range(2):
        for i in range(nv):
            cut = slice(i * lv, (i + 1) * lv)
            at = p * nv + i
            grad = dqv[cut] if p == 0 else dvkv[0, cut]
            rate = to_column(rates[at : at + 1], lv)
            back = vg[p : p + 1] * grad * rate - vraw[p, cut].astype(F32) * to_column(inner[at : at + 1], lv)
            gv[p, cut] = back.astype(BF16)

    def take_grads(c):
        landed(retr, ret_recv, 1, c)
        for j in range(VB):
            some = unpacked(retr, 1, c, j).astype(BF16)
            cut = slice(j * ga_rows, (j + 1) * ga_rows)
            for h in range(heads):
                for arr in range(2):
                    top = (2 * h + arr) * ga_rows
                    aun[arr, cut, lane_at(c, h)] = some[top : top + ga_rows]

    each_chunk(take_grads)
    stats[2, hd] = jnp.zeros((16, 128), F32)
    for p in range(2):
        for i in range(na):
            cut = slice(i * la, (i + 1) * la)
            raw = araw[p, i * la // tok : (i + 1) * la // tok].reshape(la, f).astype(F32)
            term = raw * ag[p : p + 1] * aun[p, cut].astype(F32)
            at = 2 * nv + p * na + i
            stats[2, hd, at : at + 1] = to_row(jnp.sum(term, 1, keepdims=True))
    share(2)
    inner[...] = rates[...] * rates[...] * rates[...] * shared(2) / feat_all
    for p in range(2):
        for i in range(na):
            cut = slice(i * la, (i + 1) * la)
            owned = slice(i * la // tok, (i + 1) * la // tok)
            at = 2 * nv + p * na + i
            raw = araw[p, owned].reshape(la, f).astype(F32)
            back = (
                ag[p : p + 1] * aun[p, cut].astype(F32) * to_column(rates[at : at + 1], la)
                - raw * to_column(inner[at : at + 1], la)
            )
            ga[p, owned] = back.astype(BF16).reshape(la // tok, tok, f)

    def take_outputs(c):
        landed(retr, ret_recv, 0, c)
        for j in range(VB):
            some = unpacked(retr, 0, c, j).astype(BF16)
            cut = slice(j * nb, (j + 1) * nb)
            for h in range(heads):
                top = 2 * h * ga_rows
                at = lane_at(c, h)
                oa[cut, :, at] = some[top : top + ga_rows].reshape(nb, tok, HD)
                ga[2, cut, :, at] = some[top + ga_rows : top + 2 * ga_rows].reshape(nb, tok, HD)

    each_chunk(take_outputs)

    for kind in range(2):
        for copy in video_halo(kind):
            copy.wait_send()

    def drain(c):
        edges = grad_halo(evs, evr, ev_send, ev_recv, c) + grad_halo(eas, ear, ea_send, ea_recv, c)
        for kind in range(2):
            sent(msg, a2a_send, kind, c)
            sent(ret, ret_send, kind, c)
            edges = edges + audio_halo(kind, c)
        for copy in edges:
            copy.wait_send()

    each_chunk(drain)


def store(ov, oa, gv, ga, ov_out, oa_out, gv_out, ga_out, sem):
    half = ov.shape[0] // 2
    pairs = [(oa, oa_out)]
    for i in range(2):
        rows = pl.ds(i * half, half)
        pairs += [(gv.at[p, rows], gv_out.at[p, rows]) for p in range(3)]
        pairs.append((ov.at[rows], ov_out.at[rows]))
    pairs += [(ga.at[p], ga_out.at[p]) for p in range(3)]
    copies = [
        pltpu.make_async_copy(src, dst, sem.at[i // 8, i % 8]) for i, (src, dst) in enumerate(pairs)
    ]
    for copy in copies:
        copy.start()
    for copy in copies:
        copy.wait()


def local(video_qkv, audio_qkv, video_gain, audio_gain, video_cot, audio_cot, intersection, lengths):
    n, x = lax.axis_size("tm"), lax.axis_size("head")
    f = video_qkv.shape[2]
    v_rows, a_rows = video_qkv.shape[1], n * audio_qkv.shape[2]
    ga_rows = a_rows // VB
    ae_rows, ve_rows = a_rows + 2 * ga_rows, v_rows + 2 * VBLK
    hbm = pl.BlockSpec(memory_space=pltpu.HBM)
    vmem = pl.BlockSpec(memory_space=pltpu.VMEM)
    dma = pltpu.SemaphoreType.DMA
    bf = lambda *shape: pltpu.VMEM(shape, BF16)
    f32 = lambda *shape: pltpu.VMEM(shape, F32)
    scratch = [
        f32(2, f), f32(2, f), pltpu.VMEM((2, n * n), jnp.int32), pltpu.VMEM((1, n * n), jnp.int32),
        bf(2, v_rows, f), bf(v_rows, f), bf(3, n, 4, f), bf(n, 4, f),
        bf(v_rows, f), bf(2, ve_rows, f), bf(2, CHUNKS, n, 16, HD), bf(2, CHUNKS, n, 16, HD),
        bf(a_rows, f), bf(2, ae_rows, f), bf(a_rows, f),
        f32(v_rows, f), f32(2, v_rows, f),
        bf(a_rows, f), f32(2, ae_rows, f), bf(a_rows, f),
        bf(2, 2, VBLK, f), bf(2, 2, VBLK, f), bf(2, 2, ga_rows, f), bf(2, 2, ga_rows, f),
        bf(2, CHUNKS, n, 16, HD), bf(2, CHUNKS, n, 16, HD), bf(2, a_rows, f),
        f32(VB, 3 * ga_rows, VBLK), f32(2, 4 * VBLK, 2 * ga_rows), f32(a_rows, 128),
        f32(3, x, 16, 128), f32(16, 128), f32(16, 128),
        dma((9,)), dma((3,)), dma((3,)), dma((2, 2)), dma((2, 2)),
        dma((2, CHUNKS, 2)), dma((2, CHUNKS, 2)), dma((2, CHUNKS)), dma((2, CHUNKS)),
        dma((CHUNKS, 2)), dma((CHUNKS, 2)), dma((CHUNKS, 2)), dma((CHUNKS, 2)),
        dma((2, CHUNKS)), dma((2, CHUNKS)),
    ]
    stay = lambda array: pltpu.with_memory_space_constraint(array, pltpu.HBM)
    results = pl.pallas_call(
        functools.partial(kernel, (n, x, f)),
        out_shape=(
            jax.ShapeDtypeStruct(video_cot.shape, BF16),
            jax.ShapeDtypeStruct(audio_cot.shape, BF16),
            jax.ShapeDtypeStruct(video_qkv.shape, BF16),
            jax.ShapeDtypeStruct(audio_qkv.shape, BF16),
        ),
        in_specs=[hbm] * 8,
        out_specs=(vmem, vmem, vmem, vmem),
        scratch_shapes=scratch,
        compiler_params=pltpu.CompilerParams(
            collective_id=0, has_side_effects=True, vmem_limit_bytes=40 << 20
        ),
        name="window",
    )(
        *map(stay, (video_qkv, audio_qkv, video_gain, audio_gain, video_cot, audio_cot)),
        stay(intersection.T), stay(lengths[None]),
    )
    return pl.pallas_call(
        store,
        out_shape=tuple(jax.ShapeDtypeStruct(result.shape, BF16) for result in results),
        in_specs=[vmem] * 4,
        out_specs=(hbm,) * 4,
        scratch_shapes=[dma((2, 8))],
        compiler_params=pltpu.CompilerParams(vmem_limit_bytes=16 << 20),
        name="store",
    )(*results)


def solution(mesh):
    return jax.shard_map(
        local,
        mesh=mesh,
        in_specs=(
            P(None, "tm", "head"),
            P(None, None, "tm", "head"),
            P(None, "head"),
            P(None, "head"),
            P("tm", "head"),
            P(None, "tm", "head"),
            P(),
            P(),
        ),
        out_specs=(
            P("tm", "head"),
            P(None, "tm", "head"),
            P(None, "tm", "head"),
            P(None, None, "tm", "head"),
        ),
        check_vma=False,
    )
```

```python
import functools

import jax
import jax.numpy as jnp
from jax import lax
from jax.experimental import pallas as pl
from jax.experimental.pallas import tpu as pltpu
from jax.sharding import PartitionSpec as P

HEADS = 24
HD = 128
VB = 4
VBLK = 128
CHUNKS = 3

EPSILON = 1e-06
NEGATIVE = -1e30
MESH = pl.DeviceIdType.MESH
F32 = jnp.float32
BF16 = jnp.bfloat16


def mm(a, b, ca, cb):
    return lax.dot_general(a, b, (((ca,), (cb,)), ((), ())), preferred_element_type=F32)


def attend(query, key, value, cot, bias):
    scale = HD ** (-0.5)
    scores = mm(key, query, 1, 1) * scale + bias
    exponent = jnp.exp(scores - jnp.max(scores, 0, keepdims=True))
    inverse = 1.0 / jnp.sum(exponent, 0, keepdims=True)
    probs = (exponent * inverse).astype(BF16)
    wide = probs.astype(F32)
    prob_grad = mm(value, cot, 1, 1)
    inner = jnp.sum(prob_grad * wide, 0, keepdims=True)
    score_grad = (wide * (prob_grad - inner)).astype(BF16)
    out = mm(probs, value, 0, 0)
    query_grad = mm(score_grad, key, 0, 0) * scale
    key_grad = mm(score_grad, query, 1, 0) * scale
    value_grad = mm(probs, cot, 1, 0)
    return out, query_grad, key_grad, value_grad


def iota(shape, dim):
    return lax.broadcasted_iota(jnp.int32, shape, dim)


def to_row(column):
    n = column.shape[0]
    return jnp.sum(jnp.where(iota((n, 128), 0) == iota((n, 128), 1), column, 0.0), 0, keepdims=True)


def to_column(row, n):
    return jnp.sum(jnp.where(iota((n, 128), 0) == iota((n, 128), 1), row, 0.0), 1, keepdims=True)


def kernel(
    dims,
    vq_hbm, aq_hbm, vg_hbm, ag_hbm, vc_hbm, ac_hbm, inter_hbm, lens_hbm,
    ov, oa, gv, ga,
    vg, ag, inter, lens, vraw, vcot, araw, acot, vqn, vkv, msg, win, aqn, akv, acw,
    dqv, dvkv, dqa, dakv, oaw, evs, evr, eas, ear, ret, retr, aun,
    vab, avb, live, stats, rates, inner,
    in_sem, st_send, st_recv, vh_send, vh_recv, ah_send, ah_recv,
    a2a_send, a2a_recv, ev_send, ev_recv, ea_send, ea_recv, ret_send, ret_recv,
):
    n, x, f = dims
    c_all, w = CHUNKS, f // CHUNKS
    heads = w // HD
    tok = 4
    nb = n // VB
    ga_rows = nb * tok
    a_rows = n * tok
    ae_rows = a_rows + 2 * ga_rows
    v_rows = VB * VBLK
    lv, la = min(128, v_rows), min(128, a_rows)
    nv, na = v_rows // lv, a_rows // la
    blocks = n * n
    feat_all = HEADS * HD
    me = lax.axis_index("tm")
    hd = lax.axis_index("head")
    left, right = lax.rem(me + n - 1, n), lax.rem(me + 1, n)

    barrier = pltpu.get_barrier_semaphore()
    for k in range(1, x):
        pl.semaphore_signal(barrier, inc=1, device_id={"head": lax.rem(hd + k, x)}, device_id_type=MESH)

    def greet(k, carry):
        pl.semaphore_signal(barrier, inc=1, device_id={"tm": lax.rem(me + k, n)}, device_id_type=MESH)
        return carry

    loads = [
        pltpu.make_async_copy(vq_hbm.at[pl.ds(0, 2)], vraw, in_sem.at[0]),
        pltpu.make_async_copy(aq_hbm, araw, in_sem.at[1]),
        pltpu.make_async_copy(ac_hbm, acot, in_sem.at[2]),
        pltpu.make_async_copy(vq_hbm.at[2], vkv.at[1, pl.ds(VBLK, v_rows)], in_sem.at[3]),
        pltpu.make_async_copy(vc_hbm, vcot, in_sem.at[4]),
        pltpu.make_async_copy(inter_hbm, inter, in_sem.at[5]),
        pltpu.make_async_copy(lens_hbm, lens, in_sem.at[6]),
        pltpu.make_async_copy(vg_hbm, vg, in_sem.at[7]),
        pltpu.make_async_copy(ag_hbm, ag, in_sem.at[8]),
    ]
    for load in loads:
        load.start()
    lax.fori_loop(1, n, greet, 0)

    start = me * n - nb
    count = blocks // 128
    chunk_0 = lax.rem((start + blocks) // 128, count)
    chunk_1 = lax.rem(chunk_0 + 1, count)
    rows = iota((ae_rows, 1), 0)
    block = start + lax.shift_right_logical(rows, 2)
    block = jnp.where(block < 0, block + blocks, block)
    block = jnp.where(block >= blocks, block - blocks, block)
    loads[5].wait()
    loads[6].wait()
    tables = []
    for ref, at in ((inter, 0), (inter, 1), (lens, 0)):
        column = jnp.zeros((ae_rows, 1), F32)
        for chunk in (chunk_0, chunk_1):
            lanes = pl.ds(pl.multiple_of(chunk * 128, 128), 128)
            values = ref[at : at + 1, lanes].astype(F32)
            hit = (chunk * 128 + iota((ae_rows, 128), 1)) == block
            column = column + jnp.sum(jnp.where(hit, values, 0.0), 1, keepdims=True)
        tables.append(column)
    low, high, length = tables
    is_live = jnp.bitwise_and(rows, 3).astype(F32) < length
    first = (me * VB).astype(F32)
    for b in range(VB):
        span = slice(b * ga_rows, (b + 3) * ga_rows)
        ok = (low[span] <= first + b) & (first + b <= high[span]) & is_live[span]
        vab[b] = jnp.broadcast_to(jnp.where(ok, 0.0, NEGATIVE), (3 * ga_rows, VBLK))
    pair = 2 * ga_rows
    for p in range(2):
        span = slice(ga_rows + p * pair, ga_rows + (p + 1) * pair)
        low_row = to_row(low[span])[:, :pair]
        high_row = to_row(high[span])[:, :pair]
        for e in range(4):
            at = first + (2 * p + e - 1)
            ok = (low_row <= at) & (at <= high_row)
            avb[p, e * VBLK : (e + 1) * VBLK] = jnp.broadcast_to(
                jnp.where(ok, 0.0, NEGATIVE), (VBLK, pair)
            )
    live[...] = jnp.broadcast_to(
        jnp.where(is_live[ga_rows : ga_rows + a_rows], 1.0, 0.0), (a_rows, 128)
    )

    stats[0, hd] = jnp.zeros((16, 128), F32)
    loads[1].wait()
    for p in range(2):
        for i in range(na):
            cut = slice(i * la // tok, (i + 1) * la // tok)
            raw = araw[p, cut].reshape(la, f).astype(F32)
            at = 2 * nv + p * na + i
            stats[0, hd, at : at + 1] = to_row(jnp.sum(raw * raw, 1, keepdims=True))
    loads[0].wait()
    for p in range(2):
        for i in range(nv):
            raw = vraw[p, i * lv : (i + 1) * lv].astype(F32)
            at = p * nv + i
            stats[0, hd, at : at + 1] = to_row(jnp.sum(raw * raw, 1, keepdims=True))
    for i in (2, 3, 4, 7, 8):
        loads[i].wait()

    def share(turn):
        copies = []
        for k in range(1, x):
            copies.append(
                pltpu.make_async_remote_copy(
                    stats.at[turn, hd], stats.at[turn, hd],
                    st_send.at[turn], st_recv.at[turn],
                    device_id={"head": lax.rem(hd + k, x)}, device_id_type=MESH,
                )
            )
        for copy in copies:
            copy.start()

    def shared(turn):
        some = stats.at[turn, pl.ds(0, x - 1)]
        pltpu.make_async_copy(some, some, st_recv.at[turn]).wait()
        pltpu.make_async_copy(some, some, st_send.at[turn]).wait()
        total = stats[turn, 0]
        for k in range(1, x):
            total = total + stats[turn, k]
        return total

    def edge_copy(src, dst, send, recv, to):
        return pltpu.make_async_remote_copy(
            src, dst, send, recv, device_id={"tm": to}, device_id_type=MESH
        )

    size = 4 * ga_rows
    one, two = iota((size, size), 0), iota((size, size), 1)

    def moved(row):
        arr = lax.rem(lax.div(row, tok), 4)
        return arr * ga_rows + lax.div(row, 4 * tok) * tok + lax.rem(row, tok)

    pack = jnp.where(two == moved(one), 1.0, 0.0).astype(BF16)
    unpack = jnp.where(one == moved(two), 1.0, 0.0).astype(BF16)

    def lane(c, h):
        return slice(c * w + h * HD, c * w + (h + 1) * HD)

    def put_messages(dst, kind, c, j, arrays):
        parts = [array[:, lane(c, h)] for h in range(heads) for array in arrays]
        packed = mm(pack, jnp.concatenate(parts, 0), 1, 0).astype(BF16)
        dst[kind, c, j * nb : (j + 1) * nb] = packed.reshape(nb, 16, HD)

    for j in range(VB):
        cut = slice(j * nb, (j + 1) * nb)
        arrays = araw[2, cut].reshape(ga_rows, f), acot[cut].reshape(ga_rows, f)
        for c in range(c_all):
            put_messages(msg, 0, c, j, arrays)

    pl.semaphore_wait(barrier, n - 1 + x - 1)
    share(0)

    def video_halo(kind):
        return (
            edge_copy(vkv.at[kind, pl.ds(VBLK, VBLK)], vkv.at[kind, pl.ds(VBLK + v_rows, VBLK)],
                      vh_send.at[kind, 0], vh_recv.at[kind, 0], left),
            edge_copy(vkv.at[kind, pl.ds(v_rows, VBLK)], vkv.at[kind, pl.ds(0, VBLK)],
                      vh_send.at[kind, 1], vh_recv.at[kind, 1], right),
        )

    for copy in video_halo(1):
        copy.start()

    def lanes_of(c):
        return pl.ds(pl.multiple_of(c * w, w), w)

    def spread(src, dst, send, recv):
        def chunk(kind, c):
            def one_device(k, carry):
                d = lax.rem(me + k, n)
                edge_copy(src.at[kind, c, d], dst.at[kind, c, me], send.at[kind, c], recv.at[kind, c], d).start()
                return carry

            lax.fori_loop(1, n, one_device, 0)
            pltpu.make_async_copy(src.at[kind, c, me], dst.at[kind, c, me], recv.at[kind, c]).start()

        return chunk

    def landed(dst, recv, kind, c):
        some = dst.at[kind, c]
        pltpu.make_async_copy(some, some, recv.at[kind, c]).wait()

    def sent(src, send, kind, c):
        some = src.at[kind, c, pl.ds(0, n - 1)]
        pltpu.make_async_copy(some, some, send.at[kind, c]).wait()

    spread_out = spread(msg, win, a2a_send, a2a_recv)
    spread_back = spread(ret, retr, ret_send, ret_recv)

    def each_chunk(fn):
        def body(c, carry):
            fn(c)
            return carry

        lax.fori_loop(0, c_all, body, 0)

    spread_out(0, 0)
    rates[...] = lax.rsqrt(shared(0) / feat_all + EPSILON)

    def audio_rate(p, row_at, row_count):
        i, off = divmod(row_at, la)
        at = 2 * nv + p * na + i
        return to_column(rates[at : at + 1], la)[off : off + row_count]

    for p in (1, 0):
        for i in range(nv):
            cut = slice(i * lv, (i + 1) * lv)
            at = p * nv + i
            raw = vraw[p, cut].astype(F32)
            normed = (raw * to_column(rates[at : at + 1], lv) * vg[p : p + 1]).astype(BF16)
            if p == 1:
                vkv[0, VBLK + i * lv : VBLK + (i + 1) * lv] = normed
            else:
                vqn[cut] = normed
        if p == 1:
            for copy in video_halo(0):
                copy.start()

    for j in range(VB):
        cut = slice(j * nb, (j + 1) * nb)
        arrays = []
        for p in range(2):
            raw = araw[p, cut].reshape(ga_rows, f).astype(F32)
            normed = raw * audio_rate(p, j * ga_rows, ga_rows) * ag[p : p + 1]
            arrays.append(normed.astype(BF16))
        for c in range(c_all):
            put_messages(msg, 1, c, j, arrays)
    spread_out(1, 0)

    def audio_halo(kind, c):
        lanes = lanes_of(c)
        return (
            edge_copy(akv.at[kind, pl.ds(ga_rows, ga_rows), lanes],
                      akv.at[kind, pl.ds(ga_rows + a_rows, ga_rows), lanes],
                      ah_send.at[kind, c, 0], ah_recv.at[kind, c, 0], left),
            edge_copy(akv.at[kind, pl.ds(a_rows, ga_rows), lanes],
                      akv.at[kind, pl.ds(0, ga_rows), lanes],
                      ah_send.at[kind, c, 1], ah_recv.at[kind, c, 1], right),
        )

    def grad_halo(src, dst, send, recv, c):
        lanes = lanes_of(c)
        return (
            edge_copy(src.at[0, :, :, lanes], dst.at[1, :, :, lanes], send.at[c, 0], recv.at[c, 0], left),
            edge_copy(src.at[1, :, :, lanes], dst.at[0, :, :, lanes], send.at[c, 1], recv.at[c, 1], right),
        )

    def lane_at(c, h):
        return pl.ds(pl.multiple_of(c * w + h * HD, HD), HD)

    def finish(c):
        for copy in grad_halo(eas, ear, ea_send, ea_recv, c):
            copy.wait_recv()
        for j in range(VB):
            cut = slice(j * ga_rows, (j + 1) * ga_rows)
            ext = slice((j + 1) * ga_rows, (j + 2) * ga_rows)
            parts = [], []
            for h in range(heads):
                at = lane_at(c, h)
                grads = []
                for kind in range(2):
                    total = dakv[kind, ext, at]
                    if j == 0:
                        total = total + ear[0, kind, :, at].astype(F32)
                    if j == VB - 1:
                        total = total + ear[1, kind, :, at].astype(F32)
                    grads.append(total.astype(BF16))
                parts[0].extend((oaw[cut, at], grads[1]))
                parts[1].extend((dqa[cut, at], grads[0]))
            for kind in range(2):
                packed = mm(pack, jnp.concatenate(parts[kind], 0), 1, 0).astype(BF16)
                ret[kind, c, j * nb : (j + 1) * nb] = packed.reshape(nb, 16, HD)

    def unpacked(src, kind, c, j):
        rows = src[kind, c, j * nb : (j + 1) * nb].reshape(size, HD)
        return mm(unpack, rows, 1, 0)

    def take_values(c):
        landed(win, a2a_recv, 0, c)
        for j in range(VB):
            some = unpacked(win, 0, c, j)
            cut = slice(j * ga_rows, (j + 1) * ga_rows)
            ext = slice((j + 1) * ga_rows, (j + 2) * ga_rows)
            for h in range(heads):
                at = lane_at(c, h)
                top = 2 * h * ga_rows
                akv[1, ext, at] = some[top : top + ga_rows].astype(BF16)
                cots = some[top + ga_rows : top + 2 * ga_rows]
                acw[cut, at] = jnp.where(live[cut, :1] > 0.0, cots, 0.0).astype(BF16)
        for copy in audio_halo(1, c):
            copy.start()

    take_values(0)
    spread_out(0, 1)
    for kind in range(2):
        for copy in video_halo(kind):
            copy.wait_recv()

    def chunk_work(c):
        landed(win, a2a_recv, 1, c)
        for j in range(VB):
            some = unpacked(win, 1, c, j)
            cut = slice(j * ga_rows, (j + 1) * ga_rows)
            ext = slice((j + 1) * ga_rows, (j + 2) * ga_rows)
            for h in range(heads):
                at = lane_at(c, h)
                top = 2 * h * ga_rows
                aqn[cut, at] = some[top : top + ga_rows].astype(BF16)
                akv[0, ext, at] = some[top + ga_rows : top + 2 * ga_rows].astype(BF16)
        for copy in audio_halo(0, c):
            copy.start()

        @pl.when(c < c_all - 1)
        def _():
            spread_out(1, c + 1)

        @pl.when(c == c_all - 1)
        def _():
            spread_back(0, 0)

        for h in range(heads):
            at = lane_at(c, h)
            sums = [[None] * 6, [None] * 6]
            for p in range(2):
                cut = slice(p * pair, (p + 1) * pair)
                ext = slice(2 * p * VBLK, (2 * p + 4) * VBLK)
                out, dq, dk, dv = attend(
                    aqn[cut, at], vkv[0, ext, at], vkv[1, ext, at], acw[cut, at], avb[p]
                )
                oaw[cut, at] = jnp.where(live[cut, :1] > 0.0, out, 0.0).astype(BF16)
                dqa[cut, at] = dq.astype(BF16)
                for kind, grad in enumerate((dk, dv)):
                    for e in range(4):
                        term = grad[e * VBLK : (e + 1) * VBLK]
                        old = sums[kind][2 * p + e]
                        sums[kind][2 * p + e] = term if old is None else old + term
            for kind in range(2):
                evs[0, kind, :, at] = sums[kind][0].astype(BF16)
                evs[1, kind, :, at] = sums[kind][5].astype(BF16)
                for e in range(4):
                    dvkv[kind, e * VBLK : (e + 1) * VBLK, at] = sums[kind][e + 1]
        for copy in grad_halo(evs, evr, ev_send, ev_recv, c):
            copy.start()

        @pl.when(c > 0)
        def _():
            finish(c - 1)

        @pl.when(c == 1)
        def _():
            spread_back(1, 0)

        for kind in range(2):
            for copy in audio_halo(kind, c):
                copy.wait_recv()
        for h in range(heads):
            at = lane_at(c, h)
            sums = [[None] * 6, [None] * 6]
            for b in range(VB):
                cut = slice(b * VBLK, (b + 1) * VBLK)
                ext = slice(b * ga_rows, (b + 3) * ga_rows)
                out, dq, dk, dv = attend(
                    vqn[cut, at], akv[0, ext, at], akv[1, ext, at], vcot[cut, at], vab[b]
                )
                ov[cut, at] = out.astype(BF16)
                dqv[cut, at] = dq
                for kind, grad in enumerate((dk, dv)):
                    for e in range(3):
                        term = grad[e * ga_rows : (e + 1) * ga_rows]
                        old = sums[kind][b + e]
                        sums[kind][b + e] = term if old is None else old + term
            for kind in range(2):
                eas[0, kind, :, at] = sums[kind][0].astype(BF16)
                eas[1, kind, :, at] = sums[kind][5].astype(BF16)
                for e in range(4):
                    dakv[kind, (e + 1) * ga_rows : (e + 2) * ga_rows, at] = sums[kind][e + 1]
        for copy in grad_halo(eas, ear, ea_send, ea_recv, c):
            copy.start()

        @pl.when(c < c_all - 1)
        def _():
            take_values(c + 1)

        @pl.when(c < c_all - 2)
        def _():
            spread_out(0, c + 2)

    each_chunk(chunk_work)
    spread_back(1, c_all - 2)
    finish(c_all - 1)
    spread_back(1, c_all - 1)
    for c in range(1, c_all):
        spread_back(0, c)

    def wait_edges(c):
        for copy in grad_halo(evs, evr, ev_send, ev_recv, c):
            copy.wait_recv()

    each_chunk(wait_edges)
    for kind in range(2):
        head_rows, tail_rows = slice(0, VBLK), slice(v_rows - VBLK, v_rows)
        dvkv[kind, head_rows] = dvkv[kind, head_rows] + evr[0, kind].astype(F32)
        dvkv[kind, tail_rows] = dvkv[kind, tail_rows] + evr[1, kind].astype(F32)
    stats[1, hd] = jnp.zeros((16, 128), F32)
    for p in range(2):
        for i in range(nv):
            cut = slice(i * lv, (i + 1) * lv)
            grad = dqv[cut] if p == 0 else dvkv[0, cut]
            term = vraw[p, cut].astype(F32) * vg[p : p + 1] * grad
            at = p * nv + i
            stats[1, hd, at : at + 1] = to_row(jnp.sum(term, 1, keepdims=True))
    share(1)
    for i in range(nv):
        cut = slice(i * lv, (i + 1) * lv)
        gv[2, cut] = dvkv[1, cut].astype(BF16)
    inner[...] = rates[...] * rates[...] * rates[...] * shared(1) / feat_all
    for p in range(2):
        for i in range(nv):
            cut = slice(i * lv, (i + 1) * lv)
            at = p * nv + i
            grad = dqv[cut] if p == 0 else dvkv[0, cut]
            rate = to_column(rates[at : at + 1], lv)
            back = vg[p : p + 1] * grad * rate - vraw[p, cut].astype(F32) * to_column(inner[at : at + 1], lv)
            gv[p, cut] = back.astype(BF16)

    def take_grads(c):
        landed(retr, ret_recv, 1, c)
        for j in range(VB):
            some = unpacked(retr, 1, c, j).astype(BF16)
            cut = slice(j * ga_rows, (j + 1) * ga_rows)
            for h in range(heads):
                for arr in range(2):
                    top = (2 * h + arr) * ga_rows
                    aun[arr, cut, lane_at(c, h)] = some[top : top + ga_rows]

    each_chunk(take_grads)
    stats[2, hd] = jnp.zeros((16, 128), F32)
    for p in range(2):
        for i in range(na):
            cut = slice(i * la, (i + 1) * la)
            raw = araw[p, i * la // tok : (i + 1) * la // tok].reshape(la, f).astype(F32)
            term = raw * ag[p : p + 1] * aun[p, cut].astype(F32)
            at = 2 * nv + p * na + i
            stats[2, hd, at : at + 1] = to_row(jnp.sum(term, 1, keepdims=True))
    share(2)
    inner[...] = rates[...] * rates[...] * rates[...] * shared(2) / feat_all
    for p in range(2):
        for i in range(na):
            cut = slice(i * la, (i + 1) * la)
            owned = slice(i * la // tok, (i + 1) * la // tok)
            at = 2 * nv + p * na + i
            raw = araw[p, owned].reshape(la, f).astype(F32)
            back = (
                ag[p : p + 1] * aun[p, cut].astype(F32) * to_column(rates[at : at + 1], la)
                - raw * to_column(inner[at : at + 1], la)
            )
            ga[p, owned] = back.astype(BF16).reshape(la // tok, tok, f)

    def take_outputs(c):
        landed(retr, ret_recv, 0, c)
        for j in range(VB):
            some = unpacked(retr, 0, c, j).astype(BF16)
            cut = slice(j * nb, (j + 1) * nb)
            for h in range(heads):
                top = 2 * h * ga_rows
                at = lane_at(c, h)
                oa[cut, :, at] = some[top : top + ga_rows].reshape(nb, tok, HD)
                ga[2, cut, :, at] = some[top + ga_rows : top + 2 * ga_rows].reshape(nb, tok, HD)

    each_chunk(take_outputs)

    for kind in range(2):
        for copy in video_halo(kind):
            copy.wait_send()

    def drain(c):
        edges = grad_halo(evs, evr, ev_send, ev_recv, c) + grad_halo(eas, ear, ea_send, ea_recv, c)
        for kind in range(2):
            sent(msg, a2a_send, kind, c)
            sent(ret, ret_send, kind, c)
            edges = edges + audio_halo(kind, c)
        for copy in edges:
            copy.wait_send()

    each_chunk(drain)


def store(ov, oa, gv, ga, ov_out, oa_out, gv_out, ga_out, sem):
    half = ov.shape[0] // 2
    pairs = [(oa, oa_out)]
    for i in range(2):
        rows = pl.ds(i * half, half)
        pairs += [(gv.at[p, rows], gv_out.at[p, rows]) for p in range(3)]
        pairs.append((ov.at[rows], ov_out.at[rows]))
    pairs += [(ga.at[p], ga_out.at[p]) for p in range(3)]
    copies = [
        pltpu.make_async_copy(src, dst, sem.at[i // 8, i % 8]) for i, (src, dst) in enumerate(pairs)
    ]
    for copy in copies:
        copy.start()
    for copy in copies:
        copy.wait()


def local(video_qkv, audio_qkv, video_gain, audio_gain, video_cot, audio_cot, intersection, lengths):
    n, x = lax.axis_size("tm"), lax.axis_size("head")
    f = video_qkv.shape[2]
    v_rows, a_rows = video_qkv.shape[1], n * audio_qkv.shape[2]
    ga_rows = a_rows // VB
    ae_rows, ve_rows = a_rows + 2 * ga_rows, v_rows + 2 * VBLK
    hbm = pl.BlockSpec(memory_space=pltpu.HBM)
    vmem = pl.BlockSpec(memory_space=pltpu.VMEM)
    dma = pltpu.SemaphoreType.DMA
    bf = lambda *shape: pltpu.VMEM(shape, BF16)
    f32 = lambda *shape: pltpu.VMEM(shape, F32)
    scratch = [
        f32(2, f), f32(2, f), pltpu.VMEM((2, n * n), jnp.int32), pltpu.VMEM((1, n * n), jnp.int32),
        bf(2, v_rows, f), bf(v_rows, f), bf(3, n, 4, f), bf(n, 4, f),
        bf(v_rows, f), bf(2, ve_rows, f), bf(2, CHUNKS, n, 16, HD), bf(2, CHUNKS, n, 16, HD),
        bf(a_rows, f), bf(2, ae_rows, f), bf(a_rows, f),
        f32(v_rows, f), f32(2, v_rows, f),
        bf(a_rows, f), f32(2, ae_rows, f), bf(a_rows, f),
        bf(2, 2, VBLK, f), bf(2, 2, VBLK, f), bf(2, 2, ga_rows, f), bf(2, 2, ga_rows, f),
        bf(2, CHUNKS, n, 16, HD), bf(2, CHUNKS, n, 16, HD), bf(2, a_rows, f),
        f32(VB, 3 * ga_rows, VBLK), f32(2, 4 * VBLK, 2 * ga_rows), f32(a_rows, 128),
        f32(3, x, 16, 128), f32(16, 128), f32(16, 128),
        dma((9,)), dma((3,)), dma((3,)), dma((2, 2)), dma((2, 2)),
        dma((2, CHUNKS, 2)), dma((2, CHUNKS, 2)), dma((2, CHUNKS)), dma((2, CHUNKS)),
        dma((CHUNKS, 2)), dma((CHUNKS, 2)), dma((CHUNKS, 2)), dma((CHUNKS, 2)),
        dma((2, CHUNKS)), dma((2, CHUNKS)),
    ]
    stay = lambda array: pltpu.with_memory_space_constraint(array, pltpu.HBM)
    results = pl.pallas_call(
        functools.partial(kernel, (n, x, f)),
        out_shape=(
            jax.ShapeDtypeStruct(video_cot.shape, BF16),
            jax.ShapeDtypeStruct(audio_cot.shape, BF16),
            jax.ShapeDtypeStruct(video_qkv.shape, BF16),
            jax.ShapeDtypeStruct(audio_qkv.shape, BF16),
        ),
        in_specs=[hbm] * 8,
        out_specs=(vmem, vmem, vmem, vmem),
        scratch_shapes=scratch,
        compiler_params=pltpu.CompilerParams(
            collective_id=0, has_side_effects=True, vmem_limit_bytes=40 << 20
        ),
        name="window",
    )(
        *map(stay, (video_qkv, audio_qkv, video_gain, audio_gain, video_cot, audio_cot)),
        stay(intersection.T), stay(lengths[None]),
    )
    return pl.pallas_call(
        store,
        out_shape=tuple(jax.ShapeDtypeStruct(result.shape, BF16) for result in results),
        in_specs=[vmem] * 4,
        out_specs=(hbm,) * 4,
        scratch_shapes=[dma((2, 8))],
        compiler_params=pltpu.CompilerParams(vmem_limit_bytes=16 << 20),
        name="store",
    )(*results)


def solution(mesh):
    return jax.shard_map(
        local,
        mesh=mesh,
        in_specs=(
            P(None, "tm", "head"),
            P(None, None, "tm", "head"),
            P(None, "head"),
            P(None, "head"),
            P("tm", "head"),
            P(None, "tm", "head"),
            P(),
            P(),
        ),
        out_specs=(
            P("tm", "head"),
            P(None, "tm", "head"),
            P(None, "tm", "head"),
            P(None, None, "tm", "head"),
        ),
        check_vma=False,
    )
```

```python
import functools

import jax
import jax.numpy as jnp
from jax import lax
from jax.experimental import pallas as pl
from jax.experimental.pallas import tpu as pltpu
from jax.sharding import PartitionSpec as P

HEADS = 24
HD = 128
VB = 4
VBLK = 128
CHUNKS = 3

EPSILON = 1e-06
NEGATIVE = -1e30
MESH = pl.DeviceIdType.MESH
F32 = jnp.float32
BF16 = jnp.bfloat16


def mm(a, b, ca, cb):
    return lax.dot_general(a, b, (((ca,), (cb,)), ((), ())), preferred_element_type=F32)


def attend(query, key, value, cot, bias):
    scale = HD ** (-0.5)
    scores = mm(key, query, 1, 1) * scale + bias
    exponent = jnp.exp(scores - jnp.max(scores, 0, keepdims=True))
    inverse = 1.0 / jnp.sum(exponent, 0, keepdims=True)
    probs = (exponent * inverse).astype(BF16)
    wide = probs.astype(F32)
    prob_grad = mm(value, cot, 1, 1)
    inner = jnp.sum(prob_grad * wide, 0, keepdims=True)
    score_grad = (wide * (prob_grad - inner)).astype(BF16)
    out = mm(probs, value, 0, 0)
    query_grad = mm(score_grad, key, 0, 0) * scale
    key_grad = mm(score_grad, query, 1, 0) * scale
    value_grad = mm(probs, cot, 1, 0)
    return out, query_grad, key_grad, value_grad


def iota(shape, dim):
    return lax.broadcasted_iota(jnp.int32, shape, dim)


def to_row(column):
    n = column.shape[0]
    return jnp.sum(jnp.where(iota((n, 128), 0) == iota((n, 128), 1), column, 0.0), 0, keepdims=True)


def to_column(row, n):
    return jnp.sum(jnp.where(iota((n, 128), 0) == iota((n, 128), 1), row, 0.0), 1, keepdims=True)


def kernel(
    dims,
    vq_hbm, aq_hbm, vg_hbm, ag_hbm, vc_hbm, ac_hbm, inter_hbm, lens_hbm,
    ov, oa, gv, ga,
    vg, ag, inter, lens, vraw, vcot, araw, acot, vqn, vkv, msg, win, aqn, akv, acw,
    dqv, dvkv, dqa, dakv, oaw, evs, evr, eas, ear, ret, retr, aun,
    vab, avb, live, stats, rates, inner,
    in_sem, st_send, st_recv, vh_send, vh_recv, ah_send, ah_recv,
    a2a_send, a2a_recv, ev_send, ev_recv, ea_send, ea_recv, ret_send, ret_recv,
):
    n, x, f = dims
    c_all, w = CHUNKS, f // CHUNKS
    heads = w // HD
    tok = 4
    nb = n // VB
    ga_rows = nb * tok
    a_rows = n * tok
    ae_rows = a_rows + 2 * ga_rows
    v_rows = VB * VBLK
    lv, la = min(128, v_rows), min(128, a_rows)
    nv, na = v_rows // lv, a_rows // la
    blocks = n * n
    feat_all = HEADS * HD
    me = lax.axis_index("tm")
    hd = lax.axis_index("head")
    left, right = lax.rem(me + n - 1, n), lax.rem(me + 1, n)

    barrier = pltpu.get_barrier_semaphore()
    for k in range(1, x):
        pl.semaphore_signal(barrier, inc=1, device_id={"head": lax.rem(hd + k, x)}, device_id_type=MESH)

    def greet(k, carry):
        pl.semaphore_signal(barrier, inc=1, device_id={"tm": lax.rem(me + k, n)}, device_id_type=MESH)
        return carry

    loads = [
        pltpu.make_async_copy(vq_hbm.at[pl.ds(0, 2)], vraw, in_sem.at[0]),
        pltpu.make_async_copy(aq_hbm, araw, in_sem.at[1]),
        pltpu.make_async_copy(ac_hbm, acot, in_sem.at[2]),
        pltpu.make_async_copy(vq_hbm.at[2], vkv.at[1, pl.ds(VBLK, v_rows)], in_sem.at[3]),
        pltpu.make_async_copy(vc_hbm, vcot, in_sem.at[4]),
        pltpu.make_async_copy(inter_hbm, inter, in_sem.at[5]),
        pltpu.make_async_copy(lens_hbm, lens, in_sem.at[6]),
        pltpu.make_async_copy(vg_hbm, vg, in_sem.at[7]),
        pltpu.make_async_copy(ag_hbm, ag, in_sem.at[8]),
    ]
    for load in loads:
        load.start()
    lax.fori_loop(1, n, greet, 0)

    start = me * n - nb
    count = blocks // 128
    chunk_0 = lax.rem((start + blocks) // 128, count)
    chunk_1 = lax.rem(chunk_0 + 1, count)
    rows = iota((ae_rows, 1), 0)
    block = start + lax.shift_right_logical(rows, 2)
    block = jnp.where(block < 0, block + blocks, block)
    block = jnp.where(block >= blocks, block - blocks, block)
    loads[5].wait()
    loads[6].wait()
    tables = []
    for ref, at in ((inter, 0), (inter, 1), (lens, 0)):
        column = jnp.zeros((ae_rows, 1), F32)
        for chunk in (chunk_0, chunk_1):
            lanes = pl.ds(pl.multiple_of(chunk * 128, 128), 128)
            values = ref[at : at + 1, lanes].astype(F32)
            hit = (chunk * 128 + iota((ae_rows, 128), 1)) == block
            column = column + jnp.sum(jnp.where(hit, values, 0.0), 1, keepdims=True)
        tables.append(column)
    low, high, length = tables
    is_live = jnp.bitwise_and(rows, 3).astype(F32) < length
    first = (me * VB).astype(F32)
    for b in range(VB):
        span = slice(b * ga_rows, (b + 3) * ga_rows)
        ok = (low[span] <= first + b) & (first + b <= high[span]) & is_live[span]
        vab[b] = jnp.broadcast_to(jnp.where(ok, 0.0, NEGATIVE), (3 * ga_rows, VBLK))
    pair = 2 * ga_rows
    for p in range(2):
        span = slice(ga_rows + p * pair, ga_rows + (p + 1) * pair)
        low_row = to_row(low[span])[:, :pair]
        high_row = to_row(high[span])[:, :pair]
        for e in range(4):
            at = first + (2 * p + e - 1)
            ok = (low_row <= at) & (at <= high_row)
            avb[p, e * VBLK : (e + 1) * VBLK] = jnp.broadcast_to(
                jnp.where(ok, 0.0, NEGATIVE), (VBLK, pair)
            )
    live[...] = jnp.broadcast_to(
        jnp.where(is_live[ga_rows : ga_rows + a_rows], 1.0, 0.0), (a_rows, 128)
    )

    stats[0, hd] = jnp.zeros((16, 128), F32)
    loads[1].wait()
    for p in range(2):
        for i in range(na):
            cut = slice(i * la // tok, (i + 1) * la // tok)
            raw = araw[p, cut].reshape(la, f).astype(F32)
            at = 2 * nv + p * na + i
            stats[0, hd, at : at + 1] = to_row(jnp.sum(raw * raw, 1, keepdims=True))
    loads[0].wait()
    for p in range(2):
        for i in range(nv):
            raw = vraw[p, i * lv : (i + 1) * lv].astype(F32)
            at = p * nv + i
            stats[0, hd, at : at + 1] = to_row(jnp.sum(raw * raw, 1, keepdims=True))
    for i in (2, 3, 4, 7, 8):
        loads[i].wait()

    def share(turn):
        copies = []
        for k in range(1, x):
            copies.append(
                pltpu.make_async_remote_copy(
                    stats.at[turn, hd], stats.at[turn, hd],
                    st_send.at[turn], st_recv.at[turn],
                    device_id={"head": lax.rem(hd + k, x)}, device_id_type=MESH,
                )
            )
        for copy in copies:
            copy.start()

    def shared(turn):
        some = stats.at[turn, pl.ds(0, x - 1)]
        pltpu.make_async_copy(some, some, st_recv.at[turn]).wait()
        pltpu.make_async_copy(some, some, st_send.at[turn]).wait()
        total = stats[turn, 0]
        for k in range(1, x):
            total = total + stats[turn, k]
        return total

    def edge_copy(src, dst, send, recv, to):
        return pltpu.make_async_remote_copy(
            src, dst, send, recv, device_id={"tm": to}, device_id_type=MESH
        )

    size = 4 * ga_rows
    one, two = iota((size, size), 0), iota((size, size), 1)

    def moved(row):
        arr = lax.rem(lax.div(row, tok), 4)
        return arr * ga_rows + lax.div(row, 4 * tok) * tok + lax.rem(row, tok)

    pack = jnp.where(two == moved(one), 1.0, 0.0).astype(BF16)
    unpack = jnp.where(one == moved(two), 1.0, 0.0).astype(BF16)

    def lane(c, h):
        return slice(c * w + h * HD, c * w + (h + 1) * HD)

    def put_messages(dst, kind, c, j, arrays):
        parts = [array[:, lane(c, h)] for h in range(heads) for array in arrays]
        packed = mm(pack, jnp.concatenate(parts, 0), 1, 0).astype(BF16)
        dst[kind, c, j * nb : (j + 1) * nb] = packed.reshape(nb, 16, HD)

    for j in range(VB):
        cut = slice(j * nb, (j + 1) * nb)
        arrays = araw[2, cut].reshape(ga_rows, f), acot[cut].reshape(ga_rows, f)
        for c in range(c_all):
            put_messages(msg, 0, c, j, arrays)

    pl.semaphore_wait(barrier, n - 1 + x - 1)
    share(0)

    def video_halo(kind):
        return (
            edge_copy(vkv.at[kind, pl.ds(VBLK, VBLK)], vkv.at[kind, pl.ds(VBLK + v_rows, VBLK)],
                      vh_send.at[kind, 0], vh_recv.at[kind, 0], left),
            edge_copy(vkv.at[kind, pl.ds(v_rows, VBLK)], vkv.at[kind, pl.ds(0, VBLK)],
                      vh_send.at[kind, 1], vh_recv.at[kind, 1], right),
        )

    for copy in video_halo(1):
        copy.start()

    def lanes_of(c):
        return pl.ds(pl.multiple_of(c * w, w), w)

    def spread(src, dst, send, recv):
        def chunk(kind, c):
            def one_device(k, carry):
                d = lax.rem(me + k, n)
                edge_copy(src.at[kind, c, d], dst.at[kind, c, me], send.at[kind, c], recv.at[kind, c], d).start()
                return carry

            lax.fori_loop(1, n, one_device, 0)
            pltpu.make_async_copy(src.at[kind, c, me], dst.at[kind, c, me], recv.at[kind, c]).start()

        return chunk

    def landed(dst, recv, kind, c):
        some = dst.at[kind, c]
        pltpu.make_async_copy(some, some, recv.at[kind, c]).wait()

    def sent(src, send, kind, c):
        some = src.at[kind, c, pl.ds(0, n - 1)]
        pltpu.make_async_copy(some, some, send.at[kind, c]).wait()

    spread_out = spread(msg, win, a2a_send, a2a_recv)
    spread_back = spread(ret, retr, ret_send, ret_recv)

    def each_chunk(fn):
        def body(c, carry):
            fn(c)
            return carry

        lax.fori_loop(0, c_all, body, 0)

    spread_out(0, 0)
    rates[...] = lax.rsqrt(shared(0) / feat_all + EPSILON)

    def audio_rate(p, row_at, row_count):
        i, off = divmod(row_at, la)
        at = 2 * nv + p * na + i
        return to_column(rates[at : at + 1], la)[off : off + row_count]

    for p in (1, 0):
        for i in range(nv):
            cut = slice(i * lv, (i + 1) * lv)
            at = p * nv + i
            raw = vraw[p, cut].astype(F32)
            normed = (raw * to_column(rates[at : at + 1], lv) * vg[p : p + 1]).astype(BF16)
            if p == 1:
                vkv[0, VBLK + i * lv : VBLK + (i + 1) * lv] = normed
            else:
                vqn[cut] = normed
        if p == 1:
            for copy in video_halo(0):
                copy.start()

    for j in range(VB):
        cut = slice(j * nb, (j + 1) * nb)
        arrays = []
        for p in range(2):
            raw = araw[p, cut].reshape(ga_rows, f).astype(F32)
            normed = raw * audio_rate(p, j * ga_rows, ga_rows) * ag[p : p + 1]
            arrays.append(normed.astype(BF16))
        for c in range(c_all):
            put_messages(msg, 1, c, j, arrays)
    spread_out(1, 0)

    def audio_halo(kind, c):
        lanes = lanes_of(c)
        return (
            edge_copy(akv.at[kind, pl.ds(ga_rows, ga_rows), lanes],
                      akv.at[kind, pl.ds(ga_rows + a_rows, ga_rows), lanes],
                      ah_send.at[kind, c, 0], ah_recv.at[kind, c, 0], left),
            edge_copy(akv.at[kind, pl.ds(a_rows, ga_rows), lanes],
                      akv.at[kind, pl.ds(0, ga_rows), lanes],
                      ah_send.at[kind, c, 1], ah_recv.at[kind, c, 1], right),
        )

    def grad_halo(src, dst, send, recv, c):
        lanes = lanes_of(c)
        return (
            edge_copy(src.at[0, :, :, lanes], dst.at[1, :, :, lanes], send.at[c, 0], recv.at[c, 0], left),
            edge_copy(src.at[1, :, :, lanes], dst.at[0, :, :, lanes], send.at[c, 1], recv.at[c, 1], right),
        )

    def lane_at(c, h):
        return pl.ds(pl.multiple_of(c * w + h * HD, HD), HD)

    def finish(c):
        for copy in grad_halo(eas, ear, ea_send, ea_recv, c):
            copy.wait_recv()
        for j in range(VB):
            cut = slice(j * ga_rows, (j + 1) * ga_rows)
            ext = slice((j + 1) * ga_rows, (j + 2) * ga_rows)
            parts = [], []
            for h in range(heads):
                at = lane_at(c, h)
                grads = []
                for kind in range(2):
                    total = dakv[kind, ext, at]
                    if j == 0:
                        total = total + ear[0, kind, :, at].astype(F32)
                    if j == VB - 1:
                        total = total + ear[1, kind, :, at].astype(F32)
                    grads.append(total.astype(BF16))
                parts[0].extend((oaw[cut, at], grads[1]))
                parts[1].extend((dqa[cut, at], grads[0]))
            for kind in range(2):
                packed = mm(pack, jnp.concatenate(parts[kind], 0), 1, 0).astype(BF16)
                ret[kind, c, j * nb : (j + 1) * nb] = packed.reshape(nb, 16, HD)

    def unpacked(src, kind, c, j):
        rows = src[kind, c, j * nb : (j + 1) * nb].reshape(size, HD)
        return mm(unpack, rows, 1, 0)

    def take_values(c):
        landed(win, a2a_recv, 0, c)
        for j in range(VB):
            some = unpacked(win, 0, c, j)
            cut = slice(j * ga_rows, (j + 1) * ga_rows)
            ext = slice((j + 1) * ga_rows, (j + 2) * ga_rows)
            for h in range(heads):
                at = lane_at(c, h)
                top = 2 * h * ga_rows
                akv[1, ext, at] = some[top : top + ga_rows].astype(BF16)
                cots = some[top + ga_rows : top + 2 * ga_rows]
                acw[cut, at] = jnp.where(live[cut, :1] > 0.0, cots, 0.0).astype(BF16)
        for copy in audio_halo(1, c):
            copy.start()

    take_values(0)
    spread_out(0, 1)
    for kind in range(2):
        for copy in video_halo(kind):
            copy.wait_recv()

    def chunk_work(c):
        landed(win, a2a_recv, 1, c)
        for j in range(VB):
            some = unpacked(win, 1, c, j)
            cut = slice(j * ga_rows, (j + 1) * ga_rows)
            ext = slice((j + 1) * ga_rows, (j + 2) * ga_rows)
            for h in range(heads):
                at = lane_at(c, h)
                top = 2 * h * ga_rows
                aqn[cut, at] = some[top : top + ga_rows].astype(BF16)
                akv[0, ext, at] = some[top + ga_rows : top + 2 * ga_rows].astype(BF16)
        for copy in audio_halo(0, c):
            copy.start()

        @pl.when(c < c_all - 1)
        def _():
            spread_out(1, c + 1)

        @pl.when(c == c_all - 1)
        def _():
            spread_back(0, 0)

        for h in range(heads):
            at = lane_at(c, h)
            sums = [[None] * 6, [None] * 6]
            for p in range(2):
                cut = slice(p * pair, (p + 1) * pair)
                ext = slice(2 * p * VBLK, (2 * p + 4) * VBLK)
                out, dq, dk, dv = attend(
                    aqn[cut, at], vkv[0, ext, at], vkv[1, ext, at], acw[cut, at], avb[p]
                )
                oaw[cut, at] = jnp.where(live[cut, :1] > 0.0, out, 0.0).astype(BF16)
                dqa[cut, at] = dq.astype(BF16)
                for kind, grad in enumerate((dk, dv)):
                    for e in range(4):
                        term = grad[e * VBLK : (e + 1) * VBLK]
                        old = sums[kind][2 * p + e]
                        sums[kind][2 * p + e] = term if old is None else old + term
            for kind in range(2):
                evs[0, kind, :, at] = sums[kind][0].astype(BF16)
                evs[1, kind, :, at] = sums[kind][5].astype(BF16)
                for e in range(4):
                    dvkv[kind, e * VBLK : (e + 1) * VBLK, at] = sums[kind][e + 1]
        @pl.when(c > 0)
        def _():
            finish(c - 1)

        @pl.when(c == 1)
        def _():
            spread_back(1, 0)

        for kind in range(2):
            for copy in audio_halo(kind, c):
                copy.wait_recv()
        for h in range(heads):
            at = lane_at(c, h)
            sums = [[None] * 6, [None] * 6]
            for b in range(VB):
                cut = slice(b * VBLK, (b + 1) * VBLK)
                ext = slice(b * ga_rows, (b + 3) * ga_rows)
                out, dq, dk, dv = attend(
                    vqn[cut, at], akv[0, ext, at], akv[1, ext, at], vcot[cut, at], vab[b]
                )
                ov[cut, at] = out.astype(BF16)
                dqv[cut, at] = dq
                for kind, grad in enumerate((dk, dv)):
                    for e in range(3):
                        term = grad[e * ga_rows : (e + 1) * ga_rows]
                        old = sums[kind][b + e]
                        sums[kind][b + e] = term if old is None else old + term
            for kind in range(2):
                eas[0, kind, :, at] = sums[kind][0].astype(BF16)
                eas[1, kind, :, at] = sums[kind][5].astype(BF16)
                for e in range(4):
                    dakv[kind, (e + 1) * ga_rows : (e + 2) * ga_rows, at] = sums[kind][e + 1]
        for copy in grad_halo(eas, ear, ea_send, ea_recv, c):
            copy.start()
        for copy in grad_halo(evs, evr, ev_send, ev_recv, c):
            copy.start()

        @pl.when(c < c_all - 1)
        def _():
            take_values(c + 1)

        @pl.when(c < c_all - 2)
        def _():
            spread_out(0, c + 2)

    each_chunk(chunk_work)
    spread_back(1, c_all - 2)
    finish(c_all - 1)
    spread_back(1, c_all - 1)
    for c in range(1, c_all):
        spread_back(0, c)

    def wait_edges(c):
        for copy in grad_halo(evs, evr, ev_send, ev_recv, c):
            copy.wait_recv()

    each_chunk(wait_edges)
    for kind in range(2):
        head_rows, tail_rows = slice(0, VBLK), slice(v_rows - VBLK, v_rows)
        dvkv[kind, head_rows] = dvkv[kind, head_rows] + evr[0, kind].astype(F32)
        dvkv[kind, tail_rows] = dvkv[kind, tail_rows] + evr[1, kind].astype(F32)
    stats[1, hd] = jnp.zeros((16, 128), F32)
    for p in range(2):
        for i in range(nv):
            cut = slice(i * lv, (i + 1) * lv)
            grad = dqv[cut] if p == 0 else dvkv[0, cut]
            term = vraw[p, cut].astype(F32) * vg[p : p + 1] * grad
            at = p * nv + i
            stats[1, hd, at : at + 1] = to_row(jnp.sum(term, 1, keepdims=True))
    share(1)
    for i in range(nv):
        cut = slice(i * lv, (i + 1) * lv)
        gv[2, cut] = dvkv[1, cut].astype(BF16)
    inner[...] = rates[...] * rates[...] * rates[...] * shared(1) / feat_all
    for p in range(2):
        for i in range(nv):
            cut = slice(i * lv, (i + 1) * lv)
            at = p * nv + i
            grad = dqv[cut] if p == 0 else dvkv[0, cut]
            rate = to_column(rates[at : at + 1], lv)
            back = vg[p : p + 1] * grad * rate - vraw[p, cut].astype(F32) * to_column(inner[at : at + 1], lv)
            gv[p, cut] = back.astype(BF16)

    def take_grads(c):
        landed(retr, ret_recv, 1, c)
        for j in range(VB):
            some = unpacked(retr, 1, c, j).astype(BF16)
            cut = slice(j * ga_rows, (j + 1) * ga_rows)
            for h in range(heads):
                for arr in range(2):
                    top = (2 * h + arr) * ga_rows
                    aun[arr, cut, lane_at(c, h)] = some[top : top + ga_rows]

    each_chunk(take_grads)
    stats[2, hd] = jnp.zeros((16, 128), F32)
    for p in range(2):
        for i in range(na):
            cut = slice(i * la, (i + 1) * la)
            raw = araw[p, i * la // tok : (i + 1) * la // tok].reshape(la, f).astype(F32)
            term = raw * ag[p : p + 1] * aun[p, cut].astype(F32)
            at = 2 * nv + p * na + i
            stats[2, hd, at : at + 1] = to_row(jnp.sum(term, 1, keepdims=True))
    share(2)
    inner[...] = rates[...] * rates[...] * rates[...] * shared(2) / feat_all
    for p in range(2):
        for i in range(na):
            cut = slice(i * la, (i + 1) * la)
            owned = slice(i * la // tok, (i + 1) * la // tok)
            at = 2 * nv + p * na + i
            raw = araw[p, owned].reshape(la, f).astype(F32)
            back = (
                ag[p : p + 1] * aun[p, cut].astype(F32) * to_column(rates[at : at + 1], la)
                - raw * to_column(inner[at : at + 1], la)
            )
            ga[p, owned] = back.astype(BF16).reshape(la // tok, tok, f)

    def take_outputs(c):
        landed(retr, ret_recv, 0, c)
        for j in range(VB):
            some = unpacked(retr, 0, c, j).astype(BF16)
            cut = slice(j * nb, (j + 1) * nb)
            for h in range(heads):
                top = 2 * h * ga_rows
                at = lane_at(c, h)
                oa[cut, :, at] = some[top : top + ga_rows].reshape(nb, tok, HD)
                ga[2, cut, :, at] = some[top + ga_rows : top + 2 * ga_rows].reshape(nb, tok, HD)

    each_chunk(take_outputs)

    for kind in range(2):
        for copy in video_halo(kind):
            copy.wait_send()

    def drain(c):
        edges = grad_halo(evs, evr, ev_send, ev_recv, c) + grad_halo(eas, ear, ea_send, ea_recv, c)
        for kind in range(2):
            sent(msg, a2a_send, kind, c)
            sent(ret, ret_send, kind, c)
            edges = edges + audio_halo(kind, c)
        for copy in edges:
            copy.wait_send()

    each_chunk(drain)


def store(ov, oa, gv, ga, ov_out, oa_out, gv_out, ga_out, sem):
    half = ov.shape[0] // 2
    pairs = [(oa, oa_out)]
    for i in range(2):
        rows = pl.ds(i * half, half)
        pairs += [(gv.at[p, rows], gv_out.at[p, rows]) for p in range(3)]
        pairs.append((ov.at[rows], ov_out.at[rows]))
    pairs += [(ga.at[p], ga_out.at[p]) for p in range(3)]
    copies = [
        pltpu.make_async_copy(src, dst, sem.at[i // 8, i % 8]) for i, (src, dst) in enumerate(pairs)
    ]
    for copy in copies:
        copy.start()
    for copy in copies:
        copy.wait()


def local(video_qkv, audio_qkv, video_gain, audio_gain, video_cot, audio_cot, intersection, lengths):
    n, x = lax.axis_size("tm"), lax.axis_size("head")
    f = video_qkv.shape[2]
    v_rows, a_rows = video_qkv.shape[1], n * audio_qkv.shape[2]
    ga_rows = a_rows // VB
    ae_rows, ve_rows = a_rows + 2 * ga_rows, v_rows + 2 * VBLK
    hbm = pl.BlockSpec(memory_space=pltpu.HBM)
    vmem = pl.BlockSpec(memory_space=pltpu.VMEM)
    dma = pltpu.SemaphoreType.DMA
    bf = lambda *shape: pltpu.VMEM(shape, BF16)
    f32 = lambda *shape: pltpu.VMEM(shape, F32)
    scratch = [
        f32(2, f), f32(2, f), pltpu.VMEM((2, n * n), jnp.int32), pltpu.VMEM((1, n * n), jnp.int32),
        bf(2, v_rows, f), bf(v_rows, f), bf(3, n, 4, f), bf(n, 4, f),
        bf(v_rows, f), bf(2, ve_rows, f), bf(2, CHUNKS, n, 16, HD), bf(2, CHUNKS, n, 16, HD),
        bf(a_rows, f), bf(2, ae_rows, f), bf(a_rows, f),
        f32(v_rows, f), f32(2, v_rows, f),
        bf(a_rows, f), f32(2, ae_rows, f), bf(a_rows, f),
        bf(2, 2, VBLK, f), bf(2, 2, VBLK, f), bf(2, 2, ga_rows, f), bf(2, 2, ga_rows, f),
        bf(2, CHUNKS, n, 16, HD), bf(2, CHUNKS, n, 16, HD), bf(2, a_rows, f),
        f32(VB, 3 * ga_rows, VBLK), f32(2, 4 * VBLK, 2 * ga_rows), f32(a_rows, 128),
        f32(3, x, 16, 128), f32(16, 128), f32(16, 128),
        dma((9,)), dma((3,)), dma((3,)), dma((2, 2)), dma((2, 2)),
        dma((2, CHUNKS, 2)), dma((2, CHUNKS, 2)), dma((2, CHUNKS)), dma((2, CHUNKS)),
        dma((CHUNKS, 2)), dma((CHUNKS, 2)), dma((CHUNKS, 2)), dma((CHUNKS, 2)),
        dma((2, CHUNKS)), dma((2, CHUNKS)),
    ]
    stay = lambda array: pltpu.with_memory_space_constraint(array, pltpu.HBM)
    results = pl.pallas_call(
        functools.partial(kernel, (n, x, f)),
        out_shape=(
            jax.ShapeDtypeStruct(video_cot.shape, BF16),
            jax.ShapeDtypeStruct(audio_cot.shape, BF16),
            jax.ShapeDtypeStruct(video_qkv.shape, BF16),
            jax.ShapeDtypeStruct(audio_qkv.shape, BF16),
        ),
        in_specs=[hbm] * 8,
        out_specs=(vmem, vmem, vmem, vmem),
        scratch_shapes=scratch,
        compiler_params=pltpu.CompilerParams(
            collective_id=0, has_side_effects=True, vmem_limit_bytes=40 << 20
        ),
        name="window",
    )(
        *map(stay, (video_qkv, audio_qkv, video_gain, audio_gain, video_cot, audio_cot)),
        stay(intersection.T), stay(lengths[None]),
    )
    return pl.pallas_call(
        store,
        out_shape=tuple(jax.ShapeDtypeStruct(result.shape, BF16) for result in results),
        in_specs=[vmem] * 4,
        out_specs=(hbm,) * 4,
        scratch_shapes=[dma((2, 8))],
        compiler_params=pltpu.CompilerParams(vmem_limit_bytes=16 << 20),
        name="store",
    )(*results)


def solution(mesh):
    return jax.shard_map(
        local,
        mesh=mesh,
        in_specs=(
            P(None, "tm", "head"),
            P(None, None, "tm", "head"),
            P(None, "head"),
            P(None, "head"),
            P("tm", "head"),
            P(None, "tm", "head"),
            P(),
            P(),
        ),
        out_specs=(
            P("tm", "head"),
            P(None, "tm", "head"),
            P(None, "tm", "head"),
            P(None, None, "tm", "head"),
        ),
        check_vma=False,
    )
```
